128 devices in a mesh: view: 4 (over z), tile: 32 (over y, x, core).
Axes of the slice: x: 4, y: 4, z: 4, core: 2. Of those that a mesh axis runs over, the one named last changes fastest.
Arguments:
- features: bfloat16 [8192, 128, 128], P(('view', 'tile')), may hold values from -6 to 6
- block_ids: int32 [4, 32, 128], P('view', 'tile'), may hold values from 0 to 8191, as said below
- weights: bfloat16 [4, 128, 128, 16384], P('view', 'tile'), may hold values from -0.046875 to 0.046875
- decoder: bfloat16 [1152, 512], replicated, may hold values from -0.1875 to 0.1875
- target: bfloat16 [4, 128, 128, 512], P('view', 'tile'), may hold values from -6 to 6
Outputs:
- feature_grad: float32 [8192, 128, 128], P(('view', 'tile'))
- decoder_grad: bfloat16 [1152, 512], replicated
The draws below stay inside these ranges and needn't reach their ends.
Inputs may be any that keep to these rules, and one draw needn't show every extreme that they name: `block_ids`: A block id b is held by owner b // 64 (owners numbered view-major). In each tile's list at most 2 ids belong to one owner, and some owner has exactly 2. Ids may repeat.
All inputs are finite; a program needn't handle non-finite values.
Results may differ from the reference program's by a relative error of at most 0.0075.
Values may be sent and summed in bfloat16 or wider, within the bound.
A program may use at most 128 MiB of HBM per device.

```python
import math
import jax
import jax.numpy as jnp
from jax import lax

CH = 128
OUT = 512
BLOCK = 128
K = 128
ROWS = 4
WIDTH = 128
G_DEV = 64
VIEWS = 4
OWNERS = 128
CAP = 2
NB = 8192
HEIGHT = 128
N_TILE = 32


def draw_block_ids(key, part):
    key = jax.random.fold_in(key, 11)
    keys = jax.random.split(key, VIEWS * N_TILE)

    def one_list(sub):
        first, second, third = jax.random.split(sub, 3)
        order = jax.random.permutation(first, OWNERS)
        slots = jnp.arange(K)
        quarter = OWNERS // 4
        others = OWNERS - quarter
        pick = jnp.where(slots < K // 2, slots // CAP, quarter + (slots - K // 2) % others)
        owner = order[pick]
        local = jax.random.randint(second, (K,), 0, G_DEV)
        shuffle = jax.random.permutation(third, K)
        return (owner * G_DEV + local)[shuffle]
    lists = jax.vmap(one_list)(keys)
    return lists.reshape(VIEWS, N_TILE, K).astype(jnp.int32)


def level_of(stream_key, extent, shards, least, largest):
    def one(dim, shards_of):
        heights = jax.random.uniform(jax.random.fold_in(jax.random.fold_in(stream_key, 6), dim), (shards_of,), jnp.float32, least / len(shards), largest / len(shards))
        return jnp.repeat(jnp.exp(heights), extent[dim] // shards_of).reshape((-1,) + (1,) * (len(extent) - dim - 1))

    loudness = one(*shards[0])
    for cut in shards[1:]:
        loudness = loudness * one(*cut)
    return loudness


def noise(rng, extent, deviation, most, pieces=(), kind=jnp.bfloat16):
    drawn = deviation * jax.random.normal(rng, extent, jnp.float32)
    if pieces:
        drawn = drawn * level_of(rng, extent, pieces, -0.22, 0.18)
    return jnp.clip(drawn, -most, most).astype(kind)


def setup_inputs(seed: int = 0) -> dict:
    seeds = jax.random.split(jax.random.key(seed), 6)
    features = noise(seeds[0], (NB, BLOCK, CH), 1.0, 6.0, ((0, 128),))
    block_ids = draw_block_ids(jax.random.fold_in(seeds[5], 71), 0)
    weights = noise(seeds[2], (VIEWS, HEIGHT, WIDTH, K * BLOCK), (K * BLOCK) ** -0.5, 0.046875, ((0, 4), (1, 32)))
    decoder = noise(seeds[3], (9 * CH, OUT), (9 * CH) ** -0.5, 0.1875)
    target = noise(seeds[4], (VIEWS, HEIGHT, WIDTH, OUT), 1.0, 6.0, ((0, 4), (1, 32)))
    return {"features": features, "block_ids": block_ids, "weights": weights, "decoder": decoder, "target": target}


def reference(features, block_ids, weights, decoder, target):
    flat_w = weights.reshape(VIEWS * N_TILE, ROWS * WIDTH, K * BLOCK)
    flat_ids = block_ids.reshape(VIEWS * N_TILE, K)

    def composite(pair):
        tile_w, ids = pair
        blocks = features[ids].reshape(K * BLOCK, CH)
        return jnp.dot(tile_w, blocks, preferred_element_type=jnp.float32).astype(jnp.bfloat16)
    image = lax.map(composite, (flat_w, flat_ids)).reshape(VIEWS, HEIGHT, WIDTH, CH)
    padded = jnp.pad(image, ((0, 0), (1, 1), (1, 1), (0, 0)))
    patches = jnp.concatenate([padded[:, dy:dy + HEIGHT, dx:dx + WIDTH, :] for dy in range(3) for dx in range(3)], axis=-1)
    patch_rows = patches.reshape(-1, 9 * CH)
    decoded = jnp.dot(patch_rows, decoder, preferred_element_type=jnp.float32)
    dout = (decoded - target.reshape(-1, OUT).astype(jnp.float32)).astype(jnp.bfloat16)
    weight_sum = lax.dot_general(patch_rows, dout, (((0,), (0,)), ((), ())), preferred_element_type=jnp.float32)
    decoder_grad = (weight_sum * (1.0 / math.sqrt(VIEWS * HEIGHT * WIDTH))).astype(jnp.bfloat16)
    dpatch = lax.dot_general(dout, decoder, (((1,), (1,)), ((), ())), preferred_element_type=jnp.float32)
    dpatch = dpatch.reshape(VIEWS, HEIGHT, WIDTH, 3, 3, CH)
    dpad = jnp.pad(dpatch, ((0, 0), (1, 1), (1, 1), (0, 0), (0, 0), (0, 0)))
    image_grad = jnp.zeros((VIEWS, HEIGHT, WIDTH, CH), jnp.float32)
    for dy in range(3):
        for dx in range(3):
            image_grad = image_grad + dpad[:, 2 - dy:2 - dy + HEIGHT, 2 - dx:2 - dx + WIDTH, dy, dx, :]
    grad_tiles = image_grad.astype(jnp.bfloat16).reshape(VIEWS * N_TILE, ROWS * WIDTH, CH)

    def accumulate(total, item):
        tile_w, ids, tile_g = item
        part = lax.dot_general(tile_w, tile_g, (((0,), (0,)), ((), ())), preferred_element_type=jnp.float32)
        part = lax.optimization_barrier(part.astype(jnp.bfloat16)).astype(jnp.float32)
        return (total.at[ids].add(part.reshape(K, BLOCK, CH)), None)
    feature_grad, unused = lax.scan(accumulate, jnp.zeros((NB, BLOCK, CH), jnp.float32), (flat_w, flat_ids, grad_tiles))
    return (feature_grad, decoder_grad)
```

```python
import functools
import math

import jax
import jax.numpy as jnp
from jax import lax
from jax.experimental import pallas as pl
from jax.experimental.pallas import tpu as pltpu
from jax.sharding import PartitionSpec as P

GROUP = 8


def with_halo(block, sides, width):
    for axis, dim in sides:
        count = lax.axis_size(axis)
        forward = [(i, i + 1) for i in range(count - 1)]
        backward = [(target, source) for source, target in forward]
        low = lax.ppermute(
            lax.slice_in_dim(block, block.shape[dim] - width, None, axis=dim), axis, forward
        )
        high = lax.ppermute(lax.slice_in_dim(block, 0, width, axis=dim), axis, backward)
        block = jnp.concatenate([low, block, high], axis=dim)
    return block


def pick_kernel(idx_ref, feat_ref, out_ref):
    step = pl.program_id(0)
    count = out_ref.shape[0]
    for j in range(count):
        out_ref[j] = feat_ref[idx_ref[step * count + j]]


def pick(index, features):
    count = index.shape[0]
    per = 16
    tail = features.shape[1:]
    return pl.pallas_call(
        pick_kernel,
        grid_spec=pltpu.PrefetchScalarGridSpec(
            num_scalar_prefetch=1,
            grid=(count // per,),
            in_specs=[pl.BlockSpec(memory_space=pltpu.VMEM)],
            out_specs=pl.BlockSpec((per, *tail), lambda i, idx: (i, 0, 0)),
        ),
        out_shape=jax.ShapeDtypeStruct((count, *tail), features.dtype),
        compiler_params=pltpu.CompilerParams(vmem_limit_bytes=16 << 20),
    )(index, features)


def composite_kernel(slot_ref, w_ref, *refs):
    blocks, image_ref, acc = refs[:-2], refs[-2], refs[-1]
    step = pl.program_id(0)

    @pl.when(step == 0)
    def _():
        acc[...] = jnp.zeros_like(acc)

    stacked = jnp.concatenate([b[0] for b in blocks], axis=0)
    acc[...] += jnp.dot(w_ref[...], stacked, preferred_element_type=jnp.float32)

    @pl.when(step == pl.num_programs(0) - 1)
    def _():
        image_ref[...] = acc[...].astype(image_ref.dtype)


def composite(slot, tile_w, arrived):
    pixels, listed = tile_w.shape
    _, block, chans = arrived.shape

    def at(j):
        return pl.BlockSpec((1, block, chans), lambda i, s: (s[i * GROUP + j], 0, 0))

    return pl.pallas_call(
        composite_kernel,
        grid_spec=pltpu.PrefetchScalarGridSpec(
            num_scalar_prefetch=1,
            grid=(listed // (GROUP * block),),
            in_specs=[pl.BlockSpec((pixels, GROUP * block), lambda i, s: (0, i))]
            + [at(j) for j in range(GROUP)],
            out_specs=pl.BlockSpec((pixels, chans), lambda i, s: (0, 0)),
            scratch_shapes=[pltpu.VMEM((pixels, chans), jnp.float32)],
        ),
        out_shape=jax.ShapeDtypeStruct((pixels, chans), jnp.bfloat16),
        compiler_params=pltpu.CompilerParams(vmem_limit_bytes=16 << 20),
    )(slot, tile_w, *([arrived] * GROUP))


def spread_kernel(slot_ref, w_ref, grad_ref, out_ref, buf, sems):
    step = pl.program_id(0)
    last = pl.num_programs(0) - 1
    half = lax.rem(step, 2)
    block = buf.shape[2]

    def copy(h, s, j):
        return pltpu.make_async_copy(
            buf.at[h, j], out_ref.at[slot_ref[s * GROUP + j]], sems.at[h, j]
        )

    @pl.when(step >= 2)
    def _():
        for j in range(GROUP):
            copy(half, step - 2, j).wait()

    part = lax.dot_general(
        grad_ref[...], w_ref[...], (((0,), (0,)), ((), ())), preferred_element_type=jnp.float32
    )
    for j in range(GROUP):
        buf[half, j] = part[:, j * block : (j + 1) * block].T.astype(buf.dtype)
        copy(half, step, j).start()

    @pl.when(step == last)
    def _():
        for j in range(GROUP):
            copy(1 - half, step - 1, j).wait()
            copy(half, step, j).wait()


def spread(slot, tile_w, image_grad, slots):
    pixels, listed = tile_w.shape
    chans = image_grad.shape[1]
    block = chans
    return pl.pallas_call(
        spread_kernel,
        grid_spec=pltpu.PrefetchScalarGridSpec(
            num_scalar_prefetch=1,
            grid=(listed // (GROUP * block),),
            in_specs=[
                pl.BlockSpec((pixels, GROUP * block), lambda i, s: (0, i)),
                pl.BlockSpec((pixels, chans), lambda i, s: (0, 0)),
            ],
            out_specs=pl.BlockSpec(memory_space=pl.ANY),
            scratch_shapes=[
                pltpu.VMEM((2, GROUP, block, chans), jnp.bfloat16),
                pltpu.SemaphoreType.DMA((2, GROUP)),
            ],
        ),
        out_shape=jax.ShapeDtypeStruct((slots, block, chans), jnp.bfloat16),
        compiler_params=pltpu.CompilerParams(vmem_limit_bytes=16 << 20),
    )(slot, tile_w, image_grad)


def add_kernel(idx_ref, in_ref, out_ref):
    step = pl.program_id(0)
    count = in_ref.shape[0]

    @pl.when(step == 0)
    def _():
        out_ref[...] = jnp.zeros_like(out_ref)

    for j in range(count):
        where = idx_ref[step * count + j]

        @pl.when(where >= 0)
        def _():
            out_ref[where] += in_ref[j].astype(jnp.float32)


def add_up(index, received, owned):
    count, block, chans = received.shape
    per = 16
    return pl.pallas_call(
        add_kernel,
        grid_spec=pltpu.PrefetchScalarGridSpec(
            num_scalar_prefetch=1,
            grid=(count // per,),
            in_specs=[pl.BlockSpec((per, block, chans), lambda i, idx: (i, 0, 0))],
            out_specs=pl.BlockSpec((owned, block, chans), lambda i, idx: (0, 0, 0)),
        ),
        out_shape=jax.ShapeDtypeStruct((owned, block, chans), jnp.float32),
        compiler_params=pltpu.CompilerParams(vmem_limit_bytes=24 << 20),
    )(index, received)


def body(features, block_ids, weights, decoder, target):
    n_view = lax.axis_size("view")
    n_tile = lax.axis_size("tile")
    owners = n_view * n_tile
    g_dev, block, chans = features.shape
    rows, width, listed = (weights.shape[1], weights.shape[2], weights.shape[3])
    k_len = block_ids.shape[2]
    outs = decoder.shape[1]
    cap = 2 * k_len // owners
    pixels = rows * width
    ids = block_ids[0, 0]
    owner = ids // g_dev
    local = ids - owner * g_dev
    positions = jnp.arange(k_len)
    before = positions[None, :] < positions[:, None]
    rank = jnp.sum(((owner[:, None] == owner[None, :]) & before).astype(jnp.int32), axis=1)
    slot = owner * cap + rank
    place = slot[None, :] == jnp.arange(owners * cap)[:, None]
    request = jnp.sum(jnp.where(place, local[None, :] + 1, 0), axis=1).reshape(owners, cap) - 1
    incoming = lax.all_to_all(request, ("view", "tile"), split_axis=0, concat_axis=0, tiled=True)
    incoming = incoming.reshape(-1)
    outgoing = pick(jnp.maximum(incoming, 0), features).reshape(owners, cap, block, chans)
    arrived = lax.all_to_all(outgoing, ("view", "tile"), split_axis=0, concat_axis=0, tiled=True)
    arrived = arrived.reshape(owners * cap, block, chans)
    tile_w = weights.reshape(pixels, listed)
    image = composite(slot, tile_w, arrived)
    image = image.reshape(rows, width, chans)
    rimmed = with_halo(image, (("tile", 0),), 1)
    padded = jnp.pad(rimmed, ((0, 0), (1, 1), (0, 0)))
    patches = jnp.concatenate(
        [padded[dy : dy + rows, dx : dx + width, :] for dy in range(3) for dx in range(3)], axis=-1
    )
    patch_rows = patches.reshape(pixels, 9 * chans)
    decoded = jnp.dot(patch_rows, decoder, preferred_element_type=jnp.float32)
    dout = (decoded - target.reshape(pixels, outs).astype(jnp.float32)).astype(jnp.bfloat16)
    scale = 1.0 / math.sqrt(n_view * n_tile * pixels)
    weight_part = lax.dot_general(
        patch_rows, dout, (((0,), (0,)), ((), ())), preferred_element_type=jnp.float32
    )
    decoder_grad = (lax.psum(weight_part, ("view", "tile")) * scale).astype(jnp.bfloat16)
    dout_rim = with_halo(dout.reshape(rows, width, outs), (("tile", 0),), 1)
    dout_pad = jnp.pad(dout_rim, ((0, 0), (1, 1), (0, 0)))
    dpatch = lax.dot_general(
        dout_pad.reshape((rows + 2) * (width + 2), outs),
        decoder,
        (((1,), (1,)), ((), ())),
        preferred_element_type=jnp.float32,
    )
    dpatch = dpatch.reshape(rows + 2, width + 2, 3, 3, chans)
    image_grad = jnp.zeros((rows, width, chans), jnp.float32)
    for dy in range(3):
        for dx in range(3):
            image_grad = (
                image_grad + dpatch[2 - dy : 2 - dy + rows, 2 - dx : 2 - dx + width, dy, dx, :]
            )
    image_grad = image_grad.astype(jnp.bfloat16).reshape(pixels, chans)
    returned = spread(slot, tile_w, image_grad, owners * cap)
    received = lax.all_to_all(
        returned.reshape(owners, cap, block, chans),
        ("view", "tile"),
        split_axis=0,
        concat_axis=0,
        tiled=True,
    )
    received = received.reshape(owners * cap, block, chans)
    feature_grad = add_up(incoming, received, g_dev)
    return (feature_grad, decoder_grad)


def solution(mesh):
    placed = (
        P(("view", "tile"), None, None),
        P("view", "tile", None),
        P("view", "tile", None, None),
        P(),
        P("view", "tile", None, None),
    )
    return jax.shard_map(
        body,
        mesh=mesh,
        in_specs=placed,
        out_specs=(P(("view", "tile"), None, None), P()),
        check_vma=False,
    )
```

```python
import functools
import math

import jax
import jax.numpy as jnp
from jax import lax
from jax.experimental import pallas as pl
from jax.experimental.pallas import tpu as pltpu
from jax.sharding import PartitionSpec as P

GROUP = 8


def with_halo(block, sides, width):
    for axis, dim in sides:
        count = lax.axis_size(axis)
        forward = [(i, i + 1) for i in range(count - 1)]
        backward = [(target, source) for source, target in forward]
        low = lax.ppermute(
            lax.slice_in_dim(block, block.shape[dim] - width, None, axis=dim), axis, forward
        )
        high = lax.ppermute(lax.slice_in_dim(block, 0, width, axis=dim), axis, backward)
        block = jnp.concatenate([low, block, high], axis=dim)
    return block


def pick_kernel(idx_ref, feat_ref, out_ref):
    step = pl.program_id(0)
    count = out_ref.shape[0]
    for j in range(count):
        out_ref[j] = feat_ref[idx_ref[step * count + j]]


def pick(index, features):
    count = index.shape[0]
    per = 16
    tail = features.shape[1:]
    return pl.pallas_call(
        pick_kernel,
        grid_spec=pltpu.PrefetchScalarGridSpec(
            num_scalar_prefetch=1,
            grid=(count // per,),
            in_specs=[pl.BlockSpec(memory_space=pltpu.VMEM)],
            out_specs=pl.BlockSpec((per, *tail), lambda i, idx: (i, 0, 0)),
        ),
        out_shape=jax.ShapeDtypeStruct((count, *tail), features.dtype),
        compiler_params=pltpu.CompilerParams(vmem_limit_bytes=16 << 20),
    )(index, features)


def composite_kernel(slot_ref, w_ref, *refs):
    blocks, image_ref, acc = refs[:-2], refs[-2], refs[-1]
    step = pl.program_id(0)

    @pl.when(step == 0)
    def _():
        acc[...] = jnp.zeros_like(acc)

    stacked = jnp.concatenate([b[0] for b in blocks], axis=0)
    acc[...] += jnp.dot(w_ref[...], stacked, preferred_element_type=jnp.float32)

    @pl.when(step == pl.num_programs(0) - 1)
    def _():
        image_ref[...] = acc[...].astype(image_ref.dtype)


def composite(slot, tile_w, arrived):
    pixels, listed = tile_w.shape
    _, block, chans = arrived.shape

    def at(j):
        return pl.BlockSpec((1, block, chans), lambda i, s: (s[i * GROUP + j], 0, 0))

    return pl.pallas_call(
        composite_kernel,
        grid_spec=pltpu.PrefetchScalarGridSpec(
            num_scalar_prefetch=1,
            grid=(listed // (GROUP * block),),
            in_specs=[pl.BlockSpec((pixels, GROUP * block), lambda i, s: (0, i))]
            + [at(j) for j in range(GROUP)],
            out_specs=pl.BlockSpec((pixels, chans), lambda i, s: (0, 0)),
            scratch_shapes=[pltpu.VMEM((pixels, chans), jnp.float32)],
        ),
        out_shape=jax.ShapeDtypeStruct((pixels, chans), jnp.bfloat16),
        compiler_params=pltpu.CompilerParams(vmem_limit_bytes=16 << 20),
    )(slot, tile_w, *([arrived] * GROUP))


def at_offset(step, n_view, n_tile):
    view, tile = lax.axis_index("view"), lax.axis_index("tile")
    side = n_view
    rest = step % (n_view * n_tile // 2)
    first, second, third = rest % side, (rest // side) % side, rest // (side * side)
    core = (step // (n_view * n_tile // 2) + step) % 2
    y, x, c = tile // (2 * side), (tile // 2) % side, tile % 2
    to_y = (y + first + second) % side
    to_x = (x + first + third + 2 * second) % side
    return (view + first) % side, (to_y * side + to_x) * 2 + (c + core) % 2


def give_back_kernel(
    scale, listed_ref, w_ref, grad_ref, part_ref, recv_ref, dec_ref,
    out_buf, pair_buf, mine_buf, piece_buf, send_buf, view_buf,
    send_sem, recv_sem, dec_send, dec_recv,
):
    n_view, n_tile = lax.axis_size("view"), lax.axis_size("tile")
    owners = n_view * n_tile
    chips = n_tile // 2
    view, tile = lax.axis_index("view"), lax.axis_index("tile")
    me = view * n_tile + tile
    chip, core = tile // 2, tile % 2
    block = recv_ref.shape[3]
    high = piece_buf.shape[1]
    wide = part_ref.shape[1] // block

    def remote(src, dst, send, recv, v, t):
        return pltpu.make_async_remote_copy(
            src_ref=src, dst_ref=dst, send_sem=send, recv_sem=recv,
            device_id=(v, t), device_id_type=pl.DeviceIdType.MESH,
        )

    def cols(j):
        return pl.ds(pl.multiple_of(j * block, block), block)

    def rows(j):
        return pl.ds(pl.multiple_of(j * high, 16), high)

    def to_pair(i):
        return remote(
            part_ref.at[:, cols(2 * i + 1 - core)], pair_buf.at[i],
            dec_send.at[i], dec_recv.at[i], view, 2 * chip + 1 - core,
        )

    for i in range(wide // 2):
        to_pair(i).start()

    flipped = grad_ref[...].astype(jnp.float32).T.astype(jnp.bfloat16)

    def blocks_for(lin):
        both = jnp.concatenate(
            [w_ref[:, pl.ds(listed_ref[2 * lin + r] * block, block)] for r in range(2)], axis=1
        )
        made = jnp.dot(flipped, both, preferred_element_type=jnp.float32)
        return [made[:, r * block : (r + 1) * block].T.astype(jnp.bfloat16) for r in range(2)]

    def copy(step):
        v, t = at_offset(step, n_view, n_tile)
        lin = v * n_tile + t
        return lin, remote(
            out_buf.at[lin], recv_ref.at[me], send_sem.at[step], recv_sem.at[step], v, t
        )

    def give(step, carry):
        lin, sending = copy(step)
        for r, made in enumerate(blocks_for(lin)):
            out_buf[lin, r] = made
        sending.start()
        return carry

    lead = 8
    lax.fori_loop(1, lead, give, 0)
    for i in range(wide // 2):
        to_pair(i).wait()

    def chip_sum(p_chip):
        p = 2 * p_chip + core
        r, j = p // wide, p % wide
        return part_ref[rows(r), cols(j)] + pair_buf[j // 2, rows(r), :]

    base = wide // 2

    def to_plane(step):
        to = (chip + step) % chips
        return to, remote(
            send_buf.at[to], piece_buf.at[chip],
            dec_send.at[base + step], dec_recv.at[base + step], view, 2 * to + core,
        )

    def plane_out(step, carry):
        to, sending = to_plane(step)
        send_buf[to] = chip_sum(to).astype(jnp.bfloat16)
        sending.start()
        return carry

    lax.fori_loop(1, chips, plane_out, 0)
    piece_buf[chip] = chip_sum(chip).astype(jnp.bfloat16)

    middle = owners // 4
    lax.fori_loop(lead, middle, give, 0)

    def plane_in(step, carry):
        to_plane(step)[1].wait()
        return carry

    lax.fori_loop(1, chips, plane_in, 0)
    total = piece_buf[0].astype(jnp.float32)
    for i in range(1, chips):
        total = total + piece_buf[i].astype(jnp.float32)
    mine_buf[...] = total
    view_buf[view] = total

    def to_view(step):
        return remote(
            mine_buf, view_buf.at[view],
            dec_send.at[base + chips + step], dec_recv.at[base + chips + step],
            (view + step) % n_view, tile,
        )

    for step in range(1, n_view):
        to_view(step).start()
    second = owners // 2
    lax.fori_loop(middle, second, give, 0)
    for step in range(1, n_view):
        to_view(step).wait()
    whole = view_buf[0]
    for i in range(1, n_view):
        whole = whole + view_buf[i]
    p_rows, p_cols = rows(tile // wide), cols(tile % wide)
    dec_ref[p_rows, p_cols] = (whole * scale).astype(dec_ref.dtype)

    after = base + chips + n_view

    def spread_out(step):
        to = (chip + step) % chips
        return remote(
            dec_ref.at[p_rows, p_cols], dec_ref.at[p_rows, p_cols],
            dec_send.at[after + step], dec_recv.at[after + step], view, 2 * to + core,
        )

    def spread_start(step, carry):
        spread_out(step).start()
        return carry

    lax.fori_loop(1, chips, spread_start, 0)
    lax.fori_loop(second, owners, give, 0)
    for r, made in enumerate(blocks_for(me)):
        recv_ref[me, r] = made

    def spread_wait(step, carry):
        spread_out(step).wait()
        return carry

    lax.fori_loop(1, chips, spread_wait, 0)

    def to_pair_end(i):
        part = dec_ref.at[:, cols(2 * i + core)]
        k = after + chips + i
        return remote(part, part, dec_send.at[k], dec_recv.at[k], view, 2 * chip + 1 - core)

    for i in range(wide // 2):
        to_pair_end(i).start()

    def finish(step, carry):
        copy(step)[1].wait()
        return carry

    lax.fori_loop(1, owners, finish, 0)
    for i in range(wide // 2):
        to_pair_end(i).wait()


def give_back(listed, tile_w, image_grad, weight_part, scale):
    n_view, n_tile = lax.axis_size("view"), lax.axis_size("tile")
    owners = n_view * n_tile
    chans = image_grad.shape[1]
    deep, outs = weight_part.shape
    wide = outs // chans
    high = deep * wide // n_tile
    copies = wide // 2 + n_tile // 2 + n_view + n_tile // 2 + wide // 2
    vmem = pl.BlockSpec(memory_space=pltpu.VMEM)
    return pl.pallas_call(
        functools.partial(give_back_kernel, scale),
        in_specs=[pl.BlockSpec(memory_space=pltpu.SMEM), vmem, vmem, vmem],
        out_specs=[vmem, vmem],
        out_shape=[
            jax.ShapeDtypeStruct((owners, 2, chans, chans), jnp.bfloat16),
            jax.ShapeDtypeStruct((deep, outs), jnp.bfloat16),
        ],
        scratch_shapes=[
            pltpu.VMEM((owners, 2, chans, chans), jnp.bfloat16),
            pltpu.VMEM((wide // 2, deep, chans), jnp.float32),
            pltpu.VMEM((high, chans), jnp.float32),
            pltpu.VMEM((n_tile // 2, high, chans), jnp.bfloat16),
            pltpu.VMEM((n_tile // 2, high, chans), jnp.bfloat16),
            pltpu.VMEM((n_view, high, chans), jnp.float32),
            pltpu.SemaphoreType.DMA((owners,)),
            pltpu.SemaphoreType.DMA((owners,)),
            pltpu.SemaphoreType.DMA((copies,)),
            pltpu.SemaphoreType.DMA((copies,)),
        ],
        compiler_params=pltpu.CompilerParams(has_side_effects=True, vmem_limit_bytes=56 << 20),
    )(listed, tile_w, image_grad, weight_part)


def add_kernel(idx_ref, in_ref, out_ref):
    step = pl.program_id(0)
    count = in_ref.shape[0]

    @pl.when(step == 0)
    def _():
        out_ref[...] = jnp.zeros_like(out_ref)

    for j in range(count):
        where = idx_ref[step * count + j]

        @pl.when(where >= 0)
        def _():
            out_ref[where] += in_ref[j].astype(jnp.float32)


def add_up(index, received, owned):
    count, block, chans = received.shape
    per = 16
    return pl.pallas_call(
        add_kernel,
        grid_spec=pltpu.PrefetchScalarGridSpec(
            num_scalar_prefetch=1,
            grid=(count // per,),
            in_specs=[pl.BlockSpec((per, block, chans), lambda i, idx: (i, 0, 0))],
            out_specs=pl.BlockSpec((owned, block, chans), lambda i, idx: (0, 0, 0)),
        ),
        out_shape=jax.ShapeDtypeStruct((owned, block, chans), jnp.float32),
        compiler_params=pltpu.CompilerParams(vmem_limit_bytes=24 << 20),
    )(index, received)


def body(features, block_ids, weights, decoder, target):
    n_view = lax.axis_size("view")
    n_tile = lax.axis_size("tile")
    owners = n_view * n_tile
    g_dev, block, chans = features.shape
    rows, width, listed = (weights.shape[1], weights.shape[2], weights.shape[3])
    k_len = block_ids.shape[2]
    outs = decoder.shape[1]
    cap = 2 * k_len // owners
    pixels = rows * width
    ids = block_ids[0, 0]
    owner = ids // g_dev
    local = ids - owner * g_dev
    positions = jnp.arange(k_len)
    before = positions[None, :] < positions[:, None]
    rank = jnp.sum(((owner[:, None] == owner[None, :]) & before).astype(jnp.int32), axis=1)
    slot = owner * cap + rank
    place = slot[None, :] == jnp.arange(owners * cap)[:, None]
    request = jnp.sum(jnp.where(place, local[None, :] + 1, 0), axis=1).reshape(owners, cap) - 1
    incoming = lax.all_to_all(request, ("view", "tile"), split_axis=0, concat_axis=0, tiled=True)
    incoming = incoming.reshape(-1)
    outgoing = pick(jnp.maximum(incoming, 0), features).reshape(owners, cap, block, chans)
    arrived = lax.all_to_all(outgoing, ("view", "tile"), split_axis=0, concat_axis=0, tiled=True)
    arrived = arrived.reshape(owners * cap, block, chans)
    tile_w = weights.reshape(pixels, listed)
    image = composite(slot, tile_w, arrived)
    image = image.reshape(rows, width, chans)
    rimmed = with_halo(image, (("tile", 0),), 1)
    padded = jnp.pad(rimmed, ((0, 0), (1, 1), (0, 0)))
    patches = jnp.concatenate(
        [padded[dy : dy + rows, dx : dx + width, :] for dy in range(3) for dx in range(3)], axis=-1
    )
    patch_rows = patches.reshape(pixels, 9 * chans)
    decoded = jnp.dot(patch_rows, decoder, preferred_element_type=jnp.float32)
    dout = (decoded - target.reshape(pixels, outs).astype(jnp.float32)).astype(jnp.bfloat16)
    scale = 1.0 / math.sqrt(n_view * n_tile * pixels)
    weight_part = lax.dot_general(
        patch_rows, dout, (((0,), (0,)), ((), ())), preferred_element_type=jnp.float32
    )
    dout_rim = with_halo(dout.reshape(rows, width, outs), (("tile", 0),), 1)
    dout_pad = jnp.pad(dout_rim, ((0, 0), (1, 1), (0, 0)))
    dpatch = lax.dot_general(
        dout_pad.reshape((rows + 2) * (width + 2), outs),
        decoder,
        (((1,), (1,)), ((), ())),
        preferred_element_type=jnp.float32,
    )
    dpatch = dpatch.reshape(rows + 2, width + 2, 3, 3, chans)
    image_grad = jnp.zeros((rows, width, chans), jnp.float32)
    for dy in range(3):
        for dx in range(3):
            image_grad = (
                image_grad + dpatch[2 - dy : 2 - dy + rows, 2 - dx : 2 - dx + width, dy, dx, :]
            )
    image_grad = image_grad.astype(jnp.bfloat16).reshape(pixels, chans)
    in_slot = jnp.sum(jnp.where(place, positions[None, :], 0), axis=1)
    received, decoder_grad = give_back(in_slot, tile_w, image_grad, weight_part, scale)
    received = received.reshape(owners * cap, block, chans)
    feature_grad = add_up(incoming, received, g_dev)
    return (feature_grad, decoder_grad)


def solution(mesh):
    placed = (
        P(("view", "tile"), None, None),
        P("view", "tile", None),
        P("view", "tile", None, None),
        P(),
        P("view", "tile", None, None),
    )
    return jax.shard_map(
        body,
        mesh=mesh,
        in_specs=placed,
        out_specs=(P(("view", "tile"), None, None), P()),
        check_vma=False,
    )
```

```python
import functools
import math

import jax
import jax.numpy as jnp
from jax import lax
from jax.experimental import pallas as pl
from jax.experimental.pallas import tpu as pltpu
from jax.sharding import PartitionSpec as P

GROUP = 8


def pick_kernel(idx_ref, feat_ref, out_ref):
    step = pl.program_id(0)
    count = out_ref.shape[0]
    for j in range(count):
        out_ref[j] = feat_ref[idx_ref[step * count + j]]


def pick(index, features):
    count = index.shape[0]
    per = 16
    tail = features.shape[1:]
    return pl.pallas_call(
        pick_kernel,
        grid_spec=pltpu.PrefetchScalarGridSpec(
            num_scalar_prefetch=1,
            grid=(count // per,),
            in_specs=[pl.BlockSpec(memory_space=pltpu.VMEM)],
            out_specs=pl.BlockSpec((per, *tail), lambda i, idx: (i, 0, 0)),
        ),
        out_shape=jax.ShapeDtypeStruct((count, *tail), features.dtype),
        compiler_params=pltpu.CompilerParams(vmem_limit_bytes=16 << 20),
    )(index, features)


def at_offset(step, n_view, n_tile):
    view, tile = lax.axis_index("view"), lax.axis_index("tile")
    side = n_view
    rest = step % (n_view * n_tile // 2)
    first, second, third = rest % side, (rest // side) % side, rest // (side * side)
    core = (step // (n_view * n_tile // 2) + step) % 2
    y, x, c = tile // (2 * side), (tile // 2) % side, tile % 2
    to_y = (y + first + second) % side
    to_x = (x + first + third + 2 * second) % side
    return (view + first) % side, (to_y * side + to_x) * 2 + (c + core) % 2


def train_kernel(
    scale, slot_ref, listed_ref, w_ref, arrived_ref, dec_w_ref, target_ref, recv_ref, dec_ref,
    acc, rows_buf, target_buf, part_ref,
    out_buf, pair_buf, mine_buf, piece_buf, send_buf, view_buf,
    send_sem, recv_sem, dec_send, dec_recv, halo_send, halo_recv, own_sem,
):
    n_view, n_tile = lax.axis_size("view"), lax.axis_size("tile")
    owners = n_view * n_tile
    chips = n_tile // 2
    view, tile = lax.axis_index("view"), lax.axis_index("tile")
    me = view * n_tile + tile
    chip, core = tile // 2, tile % 2
    block = recv_ref.shape[3]
    high = piece_buf.shape[1]
    wide = part_ref.shape[1] // block
    pixels = w_ref.shape[0]
    width = block

    def remote(src, dst, send, recv, v, t):
        return pltpu.make_async_remote_copy(
            src_ref=src, dst_ref=dst, send_sem=send, recv_sem=recv,
            device_id=(v, t), device_id_type=pl.DeviceIdType.MESH,
        )

    def cols(j):
        return pl.ds(pl.multiple_of(j * block, block), block)

    def rows(j):
        return pl.ds(pl.multiple_of(j * high, 16), high)

    right, left = (tile + 1) % n_tile, (tile + n_tile - 1) % n_tile
    two = 2 * width

    def halo(buf, i, src, size, dst, to):
        return remote(
            buf.at[pl.ds(src, size)], buf.at[pl.ds(dst, size)],
            halo_send.at[i], halo_recv.at[i], view, to,
        )

    target_buf[width : width + pixels, :] = target_ref[...]
    target_halos = [
        halo(target_buf, 0, pixels, width, 0, right),
        halo(target_buf, 1, width, width, width + pixels, left),
    ]
    for one in target_halos:
        one.start()

    acc[...] = jnp.zeros_like(acc)

    def add_group(i, carry):
        stacked = jnp.concatenate(
            [arrived_ref[slot_ref[i * GROUP + j]] for j in range(GROUP)], axis=0
        )
        columns = pl.ds(pl.multiple_of(i * (GROUP * block), GROUP * block), GROUP * block)
        acc[...] += jnp.dot(w_ref[:, columns], stacked, preferred_element_type=jnp.float32)
        return carry

    lax.fori_loop(0, w_ref.shape[1] // (GROUP * block), add_group, 0)
    rows_buf[two : two + pixels, :] = acc[...].astype(jnp.bfloat16)
    image_halos = [
        halo(rows_buf, 2, pixels, two, 0, right),
        halo(rows_buf, 3, two, two, two + pixels, left),
    ]
    for one in image_halos:
        one.start()
    for one in target_halos + image_halos:
        one.wait()

    padded = pixels + 4 * width
    first, last = tile == 0, tile == n_tile - 1
    place = lax.broadcasted_iota(jnp.int32, (padded, block), 0)
    outside = (first & (place < two)) | (last & (place >= two + pixels))
    image = jnp.where(outside, 0.0, rows_buf[...].astype(jnp.float32))
    column = place % width
    before = jnp.where(column == 0, 0.0, pltpu.roll(image, 1, 0))
    after_px = jnp.where(column == width - 1, 0.0, pltpu.roll(image, padded - 1, 0))
    shifted = jnp.concatenate(
        [a.astype(jnp.bfloat16) for a in (before, image, after_px)], axis=1
    )
    trans = jnp.concatenate(
        [a.T.astype(jnp.bfloat16) for a in (before, image, after_px)], axis=0
    )
    outs = dec_w_ref.shape[1]
    deep = 3 * block
    inner = pixels + two
    decoded = -target_buf[...].astype(jnp.float32)
    for dy in range(3):
        decoded = decoded + jnp.dot(
            shifted[dy * width : dy * width + inner], dec_w_ref[dy * deep : (dy + 1) * deep, :],
            preferred_element_type=jnp.float32,
        )
    place = lax.broadcasted_iota(jnp.int32, (inner, outs), 0)
    outside = (first & (place < width)) | (last & (place >= width + pixels))
    dout = jnp.where(outside, 0.0, decoded).astype(jnp.bfloat16)
    own = dout[width : width + pixels]
    for dy in range(3):
        low = (1 + dy) * width
        part_ref[dy * deep : (dy + 1) * deep, :] = jnp.dot(
            trans[:, low : low + pixels], own, preferred_element_type=jnp.float32
        )

    def to_pair(i):
        return remote(
            part_ref.at[:, cols(2 * i + 1 - core)], pair_buf.at[i],
            dec_send.at[i], dec_recv.at[i], view, 2 * chip + 1 - core,
        )

    for i in range(wide // 2):
        to_pair(i).start()

    spread = jnp.zeros((pixels, deep), jnp.float32)
    for dy in range(3):
        low = (2 - dy) * width
        spread = spread + lax.dot_general(
            dout[low : low + pixels], dec_w_ref[dy * deep : (dy + 1) * deep, :],
            (((1,), (1,)), ((), ())), preferred_element_type=jnp.float32,
        )
    column = lax.broadcasted_iota(jnp.int32, (pixels, block), 0) % width
    later = jnp.where(column == width - 1, 0.0, pltpu.roll(spread[:, :block], pixels - 1, 0))
    earlier = jnp.where(column == 0, 0.0, pltpu.roll(spread[:, 2 * block :], 1, 0))
    image_grad = (later + spread[:, block : 2 * block] + earlier).astype(jnp.bfloat16)
    flipped = image_grad.astype(jnp.float32).T.astype(jnp.bfloat16)

    def blocks_for(lin):
        both = jnp.concatenate(
            [w_ref[:, pl.ds(listed_ref[2 * lin + r] * block, block)] for r in range(2)], axis=1
        )
        made = jnp.dot(flipped, both, preferred_element_type=jnp.float32)
        return [made[:, r * block : (r + 1) * block].T.astype(jnp.bfloat16) for r in range(2)]

    def copy(step):
        v, t = at_offset(step, n_view, n_tile)
        lin = v * n_tile + t
        return lin, remote(
            out_buf.at[lin], recv_ref.at[me], send_sem.at[step], recv_sem.at[step], v, t
        )

    def give(step, carry):
        lin, sending = copy(step)
        for r, made in enumerate(blocks_for(lin)):
            out_buf[lin, r] = made
        sending.start()
        return carry

    lead = 8
    lax.fori_loop(1, lead, give, 0)
    for i in range(wide // 2):
        to_pair(i).wait()

    def chip_sum(p_chip):
        p = 2 * p_chip + core
        r, j = p // wide, p % wide
        return part_ref[rows(r), cols(j)] + pair_buf[j // 2, rows(r), :]

    base = wide // 2

    def to_plane(step):
        to = (chip + step) % chips
        return to, remote(
            send_buf.at[to], piece_buf.at[chip],
            dec_send.at[base + step], dec_recv.at[base + step], view, 2 * to + core,
        )

    def plane_out(step, carry):
        to, sending = to_plane(step)
        send_buf[to] = chip_sum(to).astype(jnp.bfloat16)
        sending.start()
        return carry

    lax.fori_loop(1, chips, plane_out, 0)
    piece_buf[chip] = chip_sum(chip).astype(jnp.bfloat16)

    middle = owners // 4
    lax.fori_loop(lead, middle, give, 0)

    def plane_in(step, carry):
        to_plane(step)[1].wait()
        return carry

    lax.fori_loop(1, chips, plane_in, 0)
    total = piece_buf[0].astype(jnp.float32)
    for i in range(1, chips):
        total = total + piece_buf[i].astype(jnp.float32)
    mine_buf[...] = total
    view_buf[view] = total

    def to_view(step):
        return remote(
            mine_buf, view_buf.at[view],
            dec_send.at[base + chips + step], dec_recv.at[base + chips + step],
            (view + step) % n_view, tile,
        )

    for step in range(1, n_view):
        to_view(step).start()
    second = owners // 2
    lax.fori_loop(middle, second, give, 0)
    for step in range(1, n_view):
        to_view(step).wait()
    whole = view_buf[0]
    for i in range(1, n_view):
        whole = whole + view_buf[i]
    p_rows, p_cols = rows(tile // wide), cols(tile % wide)
    dec_ref[p_rows, p_cols] = (whole * scale).astype(dec_ref.dtype)

    after = base + chips + n_view

    def spread_out(step):
        to = (chip + step) % chips
        return remote(
            dec_ref.at[p_rows, p_cols], dec_ref.at[p_rows, p_cols],
            dec_send.at[after + step], dec_recv.at[after + step], view, 2 * to + core,
        )

    def spread_start(step, carry):
        spread_out(step).start()
        return carry

    lax.fori_loop(1, chips, spread_start, 0)
    lax.fori_loop(second, owners, give, 0)
    for r, made in enumerate(blocks_for(me)):
        out_buf[me, r] = made
    own_copy = pltpu.make_async_copy(out_buf.at[me], recv_ref.at[me], own_sem)
    own_copy.start()

    def spread_wait(step, carry):
        spread_out(step).wait()
        return carry

    lax.fori_loop(1, chips, spread_wait, 0)

    def to_pair_end(i):
        part = dec_ref.at[:, cols(2 * i + core)]
        k = after + chips + i
        return remote(part, part, dec_send.at[k], dec_recv.at[k], view, 2 * chip + 1 - core)

    for i in range(wide // 2):
        to_pair_end(i).start()

    def finish(step, carry):
        copy(step)[1].wait()
        return carry

    lax.fori_loop(1, owners, finish, 0)
    own_copy.wait()
    for i in range(wide // 2):
        to_pair_end(i).wait()


def train(slot, listed, tile_w, arrived, decoder, target, scale):
    n_view, n_tile = lax.axis_size("view"), lax.axis_size("tile")
    owners = n_view * n_tile
    pixels = tile_w.shape[0]
    chans = arrived.shape[2]
    deep, outs = decoder.shape
    wide = outs // chans
    high = deep * wide // n_tile
    copies = wide // 2 + n_tile // 2 + n_view + n_tile // 2 + wide // 2
    vmem = pl.BlockSpec(memory_space=pltpu.VMEM)
    smem = pl.BlockSpec(memory_space=pltpu.SMEM)
    return pl.pallas_call(
        functools.partial(train_kernel, scale),
        in_specs=[smem, smem, vmem, vmem, vmem, vmem],
        out_specs=[pl.BlockSpec(memory_space=pl.ANY), vmem],
        out_shape=[
            jax.ShapeDtypeStruct((owners, 2, chans, chans), jnp.bfloat16),
            jax.ShapeDtypeStruct((deep, outs), jnp.bfloat16),
        ],
        scratch_shapes=[
            pltpu.VMEM((pixels, chans), jnp.float32),
            pltpu.VMEM((pixels + 4 * chans, chans), jnp.bfloat16),
            pltpu.VMEM((pixels + 2 * chans, outs), jnp.bfloat16),
            pltpu.VMEM((deep, outs), jnp.float32),
            pltpu.VMEM((owners, 2, chans, chans), jnp.bfloat16),
            pltpu.VMEM((wide // 2, deep, chans), jnp.float32),
            pltpu.VMEM((high, chans), jnp.float32),
            pltpu.VMEM((n_tile // 2, high, chans), jnp.bfloat16),
            pltpu.VMEM((n_tile // 2, high, chans), jnp.bfloat16),
            pltpu.VMEM((n_view, high, chans), jnp.float32),
            pltpu.SemaphoreType.DMA((owners,)),
            pltpu.SemaphoreType.DMA((owners,)),
            pltpu.SemaphoreType.DMA((copies,)),
            pltpu.SemaphoreType.DMA((copies,)),
            pltpu.SemaphoreType.DMA((4,)),
            pltpu.SemaphoreType.DMA((4,)),
            pltpu.SemaphoreType.DMA,
        ],
        compiler_params=pltpu.CompilerParams(has_side_effects=True, vmem_limit_bytes=58 << 20),
    )(slot, listed, tile_w, arrived, decoder, target)


def add_kernel(idx_ref, in_ref, out_ref, acc, sem):
    step = pl.program_id(0)
    count = in_ref.shape[0]
    owned = out_ref.shape[0]

    @pl.when(step == 0)
    def _():
        acc[...] = jnp.zeros_like(acc)

    for j in range(count):
        where = idx_ref[step * count + j]
        acc[where] += in_ref[j].astype(jnp.float32)

    @pl.when(step == pl.num_programs(0) - 1)
    def _():
        copy = pltpu.make_async_copy(acc.at[pl.ds(0, owned)], out_ref, sem)
        copy.start()
        copy.wait()


def add_up(index, received, owned):
    count, block, chans = received.shape
    per = 16
    return pl.pallas_call(
        add_kernel,
        grid_spec=pltpu.PrefetchScalarGridSpec(
            num_scalar_prefetch=1,
            grid=(count // per,),
            in_specs=[pl.BlockSpec((per, block, chans), lambda i, idx: (i, 0, 0))],
            out_specs=pl.BlockSpec(memory_space=pl.ANY),
            scratch_shapes=[
                pltpu.VMEM((owned + 1, block, chans), jnp.float32),
                pltpu.SemaphoreType.DMA,
            ],
        ),
        out_shape=jax.ShapeDtypeStruct((owned, block, chans), jnp.float32),
        compiler_params=pltpu.CompilerParams(vmem_limit_bytes=58 << 20),
    )(index, received)


def body(features, block_ids, weights, decoder, target):
    n_view = lax.axis_size("view")
    n_tile = lax.axis_size("tile")
    owners = n_view * n_tile
    g_dev, block, chans = features.shape
    rows, width, listed = (weights.shape[1], weights.shape[2], weights.shape[3])
    k_len = block_ids.shape[2]
    cap = 2 * k_len // owners
    pixels = rows * width
    ids = block_ids[0, 0]
    owner = ids // g_dev
    local = ids - owner * g_dev
    positions = jnp.arange(k_len)
    before = positions[None, :] < positions[:, None]
    rank = jnp.sum(((owner[:, None] == owner[None, :]) & before).astype(jnp.int32), axis=1)
    slot = owner * cap + rank
    place = slot[None, :] == jnp.arange(owners * cap)[:, None]
    request = jnp.sum(jnp.where(place, local[None, :] + 1, 0), axis=1).reshape(owners, cap) - 1
    incoming = lax.all_to_all(request, ("view", "tile"), split_axis=0, concat_axis=0, tiled=True)
    incoming = incoming.reshape(-1)
    outgoing = pick(jnp.maximum(incoming, 0), features).reshape(owners, cap, block, chans)
    arrived = lax.all_to_all(outgoing, ("view", "tile"), split_axis=0, concat_axis=0, tiled=True)
    arrived = arrived.reshape(owners * cap, block, chans)
    tile_w = weights.reshape(pixels, listed)
    scale = 1.0 / math.sqrt(n_view * n_tile * pixels)
    in_slot = jnp.sum(jnp.where(place, positions[None, :], 0), axis=1)
    received, decoder_grad = train(
        slot, in_slot, tile_w, arrived, decoder, target.reshape(pixels, -1), scale
    )
    received = received.reshape(owners * cap, block, chans)
    feature_grad = add_up(jnp.where(incoming < 0, g_dev, incoming), received, g_dev)
    return (feature_grad, decoder_grad)


def solution(mesh):
    placed = (
        P(("view", "tile"), None, None),
        P("view", "tile", None),
        P("view", "tile", None, None),
        P(),
        P("view", "tile", None, None),
    )
    return jax.shard_map(
        body,
        mesh=mesh,
        in_specs=placed,
        out_specs=(P(("view", "tile"), None, None), P()),
        check_vma=False,
    )
```

```python
import functools
import math

import jax
import jax.numpy as jnp
from jax import lax
from jax.experimental import pallas as pl
from jax.experimental.pallas import tpu as pltpu
from jax.sharding import PartitionSpec as P

GROUP = 8


def pick_kernel(idx_ref, feat_ref, out_ref):
    step = pl.program_id(0)
    count = out_ref.shape[0]
    for j in range(count):
        out_ref[j] = feat_ref[idx_ref[step * count + j]]


def pick(index, features):
    count = index.shape[0]
    per = 16
    tail = features.shape[1:]
    return pl.pallas_call(
        pick_kernel,
        grid_spec=pltpu.PrefetchScalarGridSpec(
            num_scalar_prefetch=1,
            grid=(count // per,),
            in_specs=[pl.BlockSpec(memory_space=pltpu.VMEM)],
            out_specs=pl.BlockSpec((per, *tail), lambda i, idx: (i, 0, 0)),
        ),
        out_shape=jax.ShapeDtypeStruct((count, *tail), features.dtype),
        compiler_params=pltpu.CompilerParams(vmem_limit_bytes=16 << 20),
    )(index, features)


def at_offset(step, n_view, n_tile):
    view, tile = lax.axis_index("view"), lax.axis_index("tile")
    side = n_view
    rest = step % (n_view * n_tile // 2)
    first, second, third = rest % side, (rest // side) % side, rest // (side * side)
    core = (step // (n_view * n_tile // 2) + step) % 2
    y, x, c = tile // (2 * side), (tile // 2) % side, tile % 2
    to_y = (y + first + second) % side
    to_x = (x + first + third + 2 * second) % side
    return (view + first) % side, (to_y * side + to_x) * 2 + (c + core) % 2


def train_kernel(
    scale, slot_ref, listed_ref, w_ref, arrived_ref, dec_w_ref, target_ref, recv_ref, dec_ref,
    acc, rows_buf, target_buf, part_ref,
    out_buf, pair_buf, mine_buf, piece_buf, send_buf, view_buf,
    send_sem, recv_sem, dec_send, dec_recv, halo_send, halo_recv, own_sem,
):
    n_view, n_tile = lax.axis_size("view"), lax.axis_size("tile")
    owners = n_view * n_tile
    chips = n_tile // 2
    view, tile = lax.axis_index("view"), lax.axis_index("tile")
    me = view * n_tile + tile
    chip, core = tile // 2, tile % 2
    block = recv_ref.shape[3]
    high = piece_buf.shape[1]
    wide = part_ref.shape[1] // block
    pixels = w_ref.shape[0]
    width = block

    def remote(src, dst, send, recv, v, t):
        return pltpu.make_async_remote_copy(
            src_ref=src, dst_ref=dst, send_sem=send, recv_sem=recv,
            device_id=(v, t), device_id_type=pl.DeviceIdType.MESH,
        )

    def cols(j):
        return pl.ds(pl.multiple_of(j * block, block), block)

    def rows(j):
        return pl.ds(pl.multiple_of(j * high, 16), high)

    right, left = (tile + 1) % n_tile, (tile + n_tile - 1) % n_tile
    two = 2 * width

    def halo(buf, i, src, size, dst, to):
        return remote(
            buf.at[pl.ds(src, size)], buf.at[pl.ds(dst, size)],
            halo_send.at[i], halo_recv.at[i], view, to,
        )

    target_buf[width : width + pixels, :] = target_ref[...]
    target_halos = [
        halo(target_buf, 0, pixels, width, 0, right),
        halo(target_buf, 1, width, width, width + pixels, left),
    ]
    for one in target_halos:
        one.start()

    acc[...] = jnp.zeros_like(acc)

    def add_group(i, carry):
        stacked = jnp.concatenate(
            [arrived_ref[slot_ref[i * GROUP + j]] for j in range(GROUP)], axis=0
        )
        columns = pl.ds(pl.multiple_of(i * (GROUP * block), GROUP * block), GROUP * block)
        acc[...] += jnp.dot(w_ref[:, columns], stacked, preferred_element_type=jnp.float32)
        return carry

    lax.fori_loop(0, w_ref.shape[1] // (GROUP * block), add_group, 0)
    rows_buf[two : two + pixels, :] = acc[...].astype(jnp.bfloat16)
    image_halos = [
        halo(rows_buf, 2, pixels, two, 0, right),
        halo(rows_buf, 3, two, two, two + pixels, left),
    ]
    for one in image_halos:
        one.start()
    for one in target_halos + image_halos:
        one.wait()

    padded = pixels + 4 * width
    first, last = tile == 0, tile == n_tile - 1
    place = lax.broadcasted_iota(jnp.int32, (padded, block), 0)
    outside = (first & (place < two)) | (last & (place >= two + pixels))
    image = jnp.where(outside, 0.0, rows_buf[...].astype(jnp.float32))
    column = place % width
    before = jnp.where(column == 0, 0.0, pltpu.roll(image, 1, 0))
    after_px = jnp.where(column == width - 1, 0.0, pltpu.roll(image, padded - 1, 0))
    shifted = jnp.concatenate(
        [a.astype(jnp.bfloat16) for a in (before, image, after_px)], axis=1
    )
    trans = jnp.concatenate(
        [a.T.astype(jnp.bfloat16) for a in (before, image, after_px)], axis=0
    )
    outs = dec_w_ref.shape[1]
    deep = 3 * block
    inner = pixels + two
    decoded = -target_buf[...].astype(jnp.float32)
    for dy in range(3):
        decoded = decoded + jnp.dot(
            shifted[dy * width : dy * width + inner], dec_w_ref[dy * deep : (dy + 1) * deep, :],
            preferred_element_type=jnp.float32,
        )
    place = lax.broadcasted_iota(jnp.int32, (inner, outs), 0)
    outside = (first & (place < width)) | (last & (place >= width + pixels))
    dout = jnp.where(outside, 0.0, decoded).astype(jnp.bfloat16)
    own = dout[width : width + pixels]
    for dy in range(3):
        low = (1 + dy) * width
        part_ref[dy * deep : (dy + 1) * deep, :] = jnp.dot(
            trans[:, low : low + pixels], own, preferred_element_type=jnp.float32
        )

    def to_pair(i):
        return remote(
            part_ref.at[:, cols(2 * i + 1 - core)], pair_buf.at[i],
            dec_send.at[i], dec_recv.at[i], view, 2 * chip + 1 - core,
        )

    for i in range(wide // 2):
        to_pair(i).start()

    spread = jnp.zeros((pixels, deep), jnp.float32)
    for dy in range(3):
        low = (2 - dy) * width
        spread = spread + lax.dot_general(
            dout[low : low + pixels], dec_w_ref[dy * deep : (dy + 1) * deep, :],
            (((1,), (1,)), ((), ())), preferred_element_type=jnp.float32,
        )
    column = lax.broadcasted_iota(jnp.int32, (pixels, block), 0) % width
    later = jnp.where(column == width - 1, 0.0, pltpu.roll(spread[:, :block], pixels - 1, 0))
    earlier = jnp.where(column == 0, 0.0, pltpu.roll(spread[:, 2 * block :], 1, 0))
    image_grad = (later + spread[:, block : 2 * block] + earlier).astype(jnp.bfloat16)
    flipped = image_grad.astype(jnp.float32).T.astype(jnp.bfloat16)

    def block_for(lin, r):
        some = w_ref[:, pl.ds(listed_ref[2 * lin + r] * block, block)]
        return jnp.dot(flipped, some, preferred_element_type=jnp.float32).T.astype(jnp.bfloat16)

    def copy(turn):
        step = turn % (owners - 1) + 1
        r = turn // (owners - 1)
        v, t = at_offset(step, n_view, n_tile)
        lin = v * n_tile + t
        return lin, r, remote(
            out_buf.at[lin, r], recv_ref.at[me, r], send_sem.at[turn], recv_sem.at[turn], v, t
        )

    def give(turn, carry):
        lin, r, sending = copy(turn)
        out_buf[lin, r] = block_for(lin, r)
        sending.start()
        return carry

    turns = 2 * (owners - 1)

    lead = 16
    lax.fori_loop(0, lead, give, 0)
    for i in range(wide // 2):
        to_pair(i).wait()

    def chip_sum(p_chip):
        p = 2 * p_chip + core
        r, j = p // wide, p % wide
        return part_ref[rows(r), cols(j)] + pair_buf[j // 2, rows(r), :]

    base = wide // 2

    def to_plane(step):
        to = (chip + step) % chips
        return to, remote(
            send_buf.at[to], piece_buf.at[chip],
            dec_send.at[base + step], dec_recv.at[base + step], view, 2 * to + core,
        )

    def plane_out(step, carry):
        to, sending = to_plane(step)
        send_buf[to] = chip_sum(to).astype(jnp.bfloat16)
        sending.start()
        return carry

    lax.fori_loop(1, chips, plane_out, 0)
    piece_buf[chip] = chip_sum(chip).astype(jnp.bfloat16)

    middle = owners // 2
    lax.fori_loop(lead, middle, give, 0)

    def plane_in(step, carry):
        to_plane(step)[1].wait()
        return carry

    lax.fori_loop(1, chips, plane_in, 0)
    total = piece_buf[0].astype(jnp.float32)
    for i in range(1, chips):
        total = total + piece_buf[i].astype(jnp.float32)
    mine_buf[...] = total
    view_buf[view] = total

    def to_view(step):
        return remote(
            mine_buf, view_buf.at[view],
            dec_send.at[base + chips + step], dec_recv.at[base + chips + step],
            (view + step) % n_view, tile,
        )

    for step in range(1, n_view):
        to_view(step).start()
    second = owners
    lax.fori_loop(middle, second, give, 0)
    for step in range(1, n_view):
        to_view(step).wait()
    whole = view_buf[0]
    for i in range(1, n_view):
        whole = whole + view_buf[i]
    p_rows, p_cols = rows(tile // wide), cols(tile % wide)
    dec_ref[p_rows, p_cols] = (whole * scale).astype(dec_ref.dtype)

    after = base + chips + n_view

    def spread_out(step):
        to = (chip + step) % chips
        return remote(
            dec_ref.at[p_rows, p_cols], dec_ref.at[p_rows, p_cols],
            dec_send.at[after + step], dec_recv.at[after + step], view, 2 * to + core,
        )

    def spread_start(step, carry):
        spread_out(step).start()
        return carry

    lax.fori_loop(1, chips, spread_start, 0)
    lax.fori_loop(second, turns, give, 0)
    for r in range(2):
        out_buf[me, r] = block_for(me, r)
    own_copy = pltpu.make_async_copy(out_buf.at[me], recv_ref.at[me], own_sem)
    own_copy.start()

    def spread_wait(step, carry):
        spread_out(step).wait()
        return carry

    lax.fori_loop(1, chips, spread_wait, 0)

    def to_pair_end(i):
        part = dec_ref.at[:, cols(2 * i + core)]
        k = after + chips + i
        return remote(part, part, dec_send.at[k], dec_recv.at[k], view, 2 * chip + 1 - core)

    for i in range(wide // 2):
        to_pair_end(i).start()

    def finish(step, carry):
        copy(step)[2].wait()
        return carry

    lax.fori_loop(0, turns, finish, 0)
    own_copy.wait()
    for i in range(wide // 2):
        to_pair_end(i).wait()


def train(slot, listed, tile_w, arrived, decoder, target, scale):
    n_view, n_tile = lax.axis_size("view"), lax.axis_size("tile")
    owners = n_view * n_tile
    pixels = tile_w.shape[0]
    chans = arrived.shape[2]
    deep, outs = decoder.shape
    wide = outs // chans
    high = deep * wide // n_tile
    copies = wide // 2 + n_tile // 2 + n_view + n_tile // 2 + wide // 2
    vmem = pl.BlockSpec(memory_space=pltpu.VMEM)
    smem = pl.BlockSpec(memory_space=pltpu.SMEM)
    return pl.pallas_call(
        functools.partial(train_kernel, scale),
        in_specs=[smem, smem, vmem, vmem, vmem, vmem],
        out_specs=[pl.BlockSpec(memory_space=pl.ANY), vmem],
        out_shape=[
            jax.ShapeDtypeStruct((owners, 2, chans, chans), jnp.bfloat16),
            jax.ShapeDtypeStruct((deep, outs), jnp.bfloat16),
        ],
        scratch_shapes=[
            pltpu.VMEM((pixels, chans), jnp.float32),
            pltpu.VMEM((pixels + 4 * chans, chans), jnp.bfloat16),
            pltpu.VMEM((pixels + 2 * chans, outs), jnp.bfloat16),
            pltpu.VMEM((deep, outs), jnp.float32),
            pltpu.VMEM((owners, 2, chans, chans), jnp.bfloat16),
            pltpu.VMEM((wide // 2, deep, chans), jnp.float32),
            pltpu.VMEM((high, chans), jnp.float32),
            pltpu.VMEM((n_tile // 2, high, chans), jnp.bfloat16),
            pltpu.VMEM((n_tile // 2, high, chans), jnp.bfloat16),
            pltpu.VMEM((n_view, high, chans), jnp.float32),
            pltpu.SemaphoreType.DMA((2 * owners,)),
            pltpu.SemaphoreType.DMA((2 * owners,)),
            pltpu.SemaphoreType.DMA((copies,)),
            pltpu.SemaphoreType.DMA((copies,)),
            pltpu.SemaphoreType.DMA((4,)),
            pltpu.SemaphoreType.DMA((4,)),
            pltpu.SemaphoreType.DMA,
        ],
        compiler_params=pltpu.CompilerParams(has_side_effects=True, vmem_limit_bytes=58 << 20),
    )(slot, listed, tile_w, arrived, decoder, target)


def add_kernel(idx_ref, in_ref, dec_in_ref, out_ref, dec_out_ref, buf, acc, dec_buf, in_sem, out_sem, dec_sem):
    count = in_ref.shape[0]
    owned = out_ref.shape[0]
    loads, stores = in_sem.shape[0], out_sem.shape[0]
    per, back = count // loads, owned // stores

    def load(i):
        return pltpu.make_async_copy(
            in_ref.at[pl.ds(i * per, per)], buf.at[pl.ds(i * per, per)], in_sem.at[i]
        )

    def store(i):
        return pltpu.make_async_copy(
            acc.at[pl.ds(i * back, back)], out_ref.at[pl.ds(i * back, back)], out_sem.at[i]
        )

    for i in range(loads):
        load(i).start()
    dec_in = pltpu.make_async_copy(dec_in_ref, dec_buf, dec_sem.at[0])
    dec_in.start()
    acc[...] = jnp.zeros_like(acc)

    for i in range(loads):
        load(i).wait()

        def one(j, carry):
            where = idx_ref[j]

            @pl.when(where >= 0)
            def _():
                acc[where] += buf[j].astype(jnp.float32)

            return carry

        lax.fori_loop(i * per, (i + 1) * per, one, 0, unroll=8)

    for i in range(stores):
        store(i).start()
    dec_in.wait()
    dec_out = pltpu.make_async_copy(dec_buf, dec_out_ref, dec_sem.at[1])
    dec_out.start()
    for i in range(stores):
        store(i).wait()
    dec_out.wait()


def add_up(index, received, decoder_grad, owned):
    count, block, chans = received.shape
    loads, stores = 16, 8
    hbm = pl.BlockSpec(memory_space=pl.ANY)
    return pl.pallas_call(
        add_kernel,
        in_specs=[pl.BlockSpec(memory_space=pltpu.SMEM), hbm, hbm],
        out_specs=[hbm, hbm],
        scratch_shapes=[
            pltpu.VMEM((count, block, chans), received.dtype),
            pltpu.VMEM((owned, block, chans), jnp.float32),
            pltpu.VMEM(decoder_grad.shape, decoder_grad.dtype),
            pltpu.SemaphoreType.DMA((loads,)),
            pltpu.SemaphoreType.DMA((stores,)),
            pltpu.SemaphoreType.DMA((2,)),
        ],
        out_shape=[
            jax.ShapeDtypeStruct((owned, block, chans), jnp.float32),
            jax.ShapeDtypeStruct(decoder_grad.shape, decoder_grad.dtype),
        ],
        compiler_params=pltpu.CompilerParams(vmem_limit_bytes=56 << 20),
    )(index, received, decoder_grad)


def body(features, block_ids, weights, decoder, target):
    n_view = lax.axis_size("view")
    n_tile = lax.axis_size("tile")
    owners = n_view * n_tile
    g_dev, block, chans = features.shape
    rows, width, listed = (weights.shape[1], weights.shape[2], weights.shape[3])
    k_len = block_ids.shape[2]
    cap = 2 * k_len // owners
    pixels = rows * width
    ids = block_ids[0, 0]
    owner = ids // g_dev
    local = ids - owner * g_dev
    positions = jnp.arange(k_len)
    before = positions[None, :] < positions[:, None]
    rank = jnp.sum(((owner[:, None] == owner[None, :]) & before).astype(jnp.int32), axis=1)
    slot = owner * cap + rank
    place = slot[None, :] == jnp.arange(owners * cap)[:, None]
    request = jnp.sum(jnp.where(place, local[None, :] + 1, 0), axis=1).reshape(owners, cap) - 1
    incoming = lax.all_to_all(request, ("view", "tile"), split_axis=0, concat_axis=0, tiled=True)
    incoming = incoming.reshape(-1)
    outgoing = pick(jnp.maximum(incoming, 0), features).reshape(owners, cap, block, chans)
    arrived = lax.all_to_all(outgoing, ("view", "tile"), split_axis=0, concat_axis=0, tiled=True)
    arrived = arrived.reshape(owners * cap, block, chans)
    tile_w = weights.reshape(pixels, listed)
    scale = 1.0 / math.sqrt(n_view * n_tile * pixels)
    in_slot = jnp.sum(jnp.where(place, positions[None, :], 0), axis=1)
    received, decoder_grad = train(
        slot, in_slot, tile_w, arrived, decoder, target.reshape(pixels, -1), scale
    )
    received = received.reshape(owners * cap, block, chans)
    return tuple(add_up(incoming, received, decoder_grad, g_dev))


def solution(mesh):
    placed = (
        P(("view", "tile"), None, None),
        P("view", "tile", None),
        P("view", "tile", None, None),
        P(),
        P("view", "tile", None, None),
    )
    return jax.shard_map(
        body,
        mesh=mesh,
        in_specs=placed,
        out_specs=(P(("view", "tile"), None, None), P()),
        check_vma=False,
    )
```

```python
import functools
import math

import jax
import jax.numpy as jnp
from jax import lax
from jax.experimental import pallas as pl
from jax.experimental.pallas import tpu as pltpu
from jax.sharding import PartitionSpec as P

GROUP = 8


def pick_kernel(idx_ref, feat_ref, out_ref):
    step = pl.program_id(0)
    count = out_ref.shape[0]
    for j in range(count):
        out_ref[j] = feat_ref[idx_ref[step * count + j]]


def pick(index, features):
    count = index.shape[0]
    per = 16
    tail = features.shape[1:]
    return pl.pallas_call(
        pick_kernel,
        grid_spec=pltpu.PrefetchScalarGridSpec(
            num_scalar_prefetch=1,
            grid=(count // per,),
            in_specs=[pl.BlockSpec(memory_space=pltpu.VMEM)],
            out_specs=pl.BlockSpec((per, *tail), lambda i, idx: (i, 0, 0)),
        ),
        out_shape=jax.ShapeDtypeStruct((count, *tail), features.dtype),
        compiler_params=pltpu.CompilerParams(vmem_limit_bytes=16 << 20),
    )(index, features)


def at_offset(step, n_view, n_tile):
    view, tile = lax.axis_index("view"), lax.axis_index("tile")
    side = n_view
    rest = step % (n_view * n_tile // 2)
    first, second, third = rest % side, (rest // side) % side, rest // (side * side)
    core = (step // (n_view * n_tile // 2) + step) % 2
    y, x, c = tile // (2 * side), (tile // 2) % side, tile % 2
    to_y = (y + first + second) % side
    to_x = (x + first + third + 2 * second) % side
    return (view + first) % side, (to_y * side + to_x) * 2 + (c + core) % 2


def train_kernel(
    scale, slot_ref, listed_ref, w_hbm, arrived_hbm, dec_w_hbm, target_hbm, recv_ref, dec_ref,
    w_ref, arrived_ref, dec_w_ref, acc, rows_buf, target_buf, part_ref,
    out_buf, pair_buf, mine_buf, piece_buf, send_buf, view_buf,
    send_sem, recv_sem, dec_send, dec_recv, halo_send, halo_recv, own_sem,
    block_sem, weight_sem, other_sem,
):
    n_view, n_tile = lax.axis_size("view"), lax.axis_size("tile")
    owners = n_view * n_tile
    chips = n_tile // 2
    view, tile = lax.axis_index("view"), lax.axis_index("tile")
    me = view * n_tile + tile
    chip, core = tile // 2, tile % 2
    block = recv_ref.shape[3]
    high = piece_buf.shape[1]
    wide = part_ref.shape[1] // block
    pixels = w_ref.shape[0]
    width = block

    def remote(src, dst, send, recv, v, t):
        return pltpu.make_async_remote_copy(
            src_ref=src, dst_ref=dst, send_sem=send, recv_sem=recv,
            device_id=(v, t), device_id_type=pl.DeviceIdType.MESH,
        )

    def cols(j):
        return pl.ds(pl.multiple_of(j * block, block), block)

    def rows(j):
        return pl.ds(pl.multiple_of(j * high, 16), high)

    group = GROUP * block
    groups = w_ref.shape[1] // group
    few = arrived_ref.shape[0] // block_sem.shape[0]

    def block_load(i):
        part = pl.ds(i * few, few)
        return pltpu.make_async_copy(arrived_hbm.at[part], arrived_ref.at[part], block_sem.at[i])

    def weight_load(i):
        part = pl.ds(pl.multiple_of(i * group, group), group)
        return pltpu.make_async_copy(w_hbm.at[:, part], w_ref.at[:, part], weight_sem.at[i])

    others = [
        pltpu.make_async_copy(dec_w_hbm, dec_w_ref, other_sem.at[0]),
        pltpu.make_async_copy(target_hbm, target_buf.at[pl.ds(width, pixels)], other_sem.at[1]),
    ]
    for i in range(block_sem.shape[0]):
        block_load(i).start()
    for i in range(groups):
        weight_load(i).start()
    for one in others:
        one.start()

    barrier = pltpu.get_barrier_semaphore()

    def greet(step, carry):
        v = lax.rem(view + lax.div(step, n_tile), n_view)
        t = lax.rem(tile + lax.rem(step, n_tile), n_tile)
        pl.semaphore_signal(
            barrier, inc=1, device_id=(v, t), device_id_type=pl.DeviceIdType.MESH
        )
        return carry

    lax.fori_loop(1, owners, greet, 0)

    right, left = (tile + 1) % n_tile, (tile + n_tile - 1) % n_tile
    two = 2 * width

    def halo(buf, i, src, size, dst, to):
        return remote(
            buf.at[pl.ds(src, size)], buf.at[pl.ds(dst, size)],
            halo_send.at[i], halo_recv.at[i], view, to,
        )

    target_halos = [
        halo(target_buf, 0, pixels, width, 0, right),
        halo(target_buf, 1, width, width, width + pixels, left),
    ]
    acc[...] = jnp.zeros_like(acc)
    for i in range(block_sem.shape[0]):
        block_load(i).wait()

    def add_group(i, carry):
        weight_load(i).wait()
        stacked = jnp.concatenate(
            [arrived_ref[slot_ref[i * GROUP + j]] for j in range(GROUP)], axis=0
        )
        columns = pl.ds(pl.multiple_of(i * group, group), group)
        acc[...] += jnp.dot(w_ref[:, columns], stacked, preferred_element_type=jnp.float32)
        return carry

    lax.fori_loop(0, groups, add_group, 0)
    for one in others:
        one.wait()
    rows_buf[two : two + pixels, :] = acc[...].astype(jnp.bfloat16)
    image_halos = [
        halo(rows_buf, 2, pixels, two, 0, right),
        halo(rows_buf, 3, two, two, two + pixels, left),
    ]
    pl.semaphore_wait(barrier, owners - 1)
    for one in image_halos + target_halos:
        one.start()
    for one in image_halos + target_halos:
        one.wait()

    padded = pixels + 4 * width
    first, last = tile == 0, tile == n_tile - 1
    place = lax.broadcasted_iota(jnp.int32, (padded, block), 0)
    outside = (first & (place < two)) | (last & (place >= two + pixels))
    image = jnp.where(outside, 0.0, rows_buf[...].astype(jnp.float32))
    column = place % width
    before = jnp.where(column == 0, 0.0, pltpu.roll(image, 1, 0))
    after_px = jnp.where(column == width - 1, 0.0, pltpu.roll(image, padded - 1, 0))
    shifted = jnp.concatenate(
        [a.astype(jnp.bfloat16) for a in (before, image, after_px)], axis=1
    )
    trans = jnp.concatenate(
        [a.T.astype(jnp.bfloat16) for a in (before, image, after_px)], axis=0
    )
    outs = dec_w_ref.shape[1]
    deep = 3 * block
    inner = pixels + two
    decoded = -target_buf[...].astype(jnp.float32)
    for dy in range(3):
        decoded = decoded + jnp.dot(
            shifted[dy * width : dy * width + inner], dec_w_ref[dy * deep : (dy + 1) * deep, :],
            preferred_element_type=jnp.float32,
        )
    place = lax.broadcasted_iota(jnp.int32, (inner, outs), 0)
    outside = (first & (place < width)) | (last & (place >= width + pixels))
    dout = jnp.where(outside, 0.0, decoded).astype(jnp.bfloat16)
    own = dout[width : width + pixels]
    for dy in range(3):
        low = (1 + dy) * width
        part_ref[dy * deep : (dy + 1) * deep, :] = jnp.dot(
            trans[:, low : low + pixels], own, preferred_element_type=jnp.float32
        )

    def to_pair(i):
        return remote(
            part_ref.at[:, cols(2 * i + 1 - core)], pair_buf.at[i],
            dec_send.at[i], dec_recv.at[i], view, 2 * chip + 1 - core,
        )

    for i in range(wide // 2):
        to_pair(i).start()

    spread = jnp.zeros((pixels, deep), jnp.float32)
    for dy in range(3):
        low = (2 - dy) * width
        spread = spread + lax.dot_general(
            dout[low : low + pixels], dec_w_ref[dy * deep : (dy + 1) * deep, :],
            (((1,), (1,)), ((), ())), preferred_element_type=jnp.float32,
        )
    column = lax.broadcasted_iota(jnp.int32, (pixels, block), 0) % width
    later = jnp.where(column == width - 1, 0.0, pltpu.roll(spread[:, :block], pixels - 1, 0))
    earlier = jnp.where(column == 0, 0.0, pltpu.roll(spread[:, 2 * block :], 1, 0))
    image_grad = (later + spread[:, block : 2 * block] + earlier).astype(jnp.bfloat16)
    flipped = image_grad.astype(jnp.float32).T.astype(jnp.bfloat16)

    def block_for(lin, r):
        some = w_ref[:, pl.ds(listed_ref[2 * lin + r] * block, block)]
        return jnp.dot(flipped, some, preferred_element_type=jnp.float32).T.astype(jnp.bfloat16)

    def copy(turn):
        step = turn % (owners - 1) + 1
        r = turn // (owners - 1)
        v, t = at_offset(step, n_view, n_tile)
        lin = v * n_tile + t
        return lin, r, remote(
            out_buf.at[lin, r], recv_ref.at[me, r], send_sem.at[turn], recv_sem.at[turn], v, t
        )

    def give(turn, carry):
        lin, r, sending = copy(turn)
        out_buf[lin, r] = block_for(lin, r)
        sending.start()
        return carry

    turns = 2 * (owners - 1)

    lead = 16
    lax.fori_loop(0, lead, give, 0)
    for i in range(wide // 2):
        to_pair(i).wait()

    def chip_sum(p_chip):
        p = 2 * p_chip + core
        r, j = p // wide, p % wide
        return part_ref[rows(r), cols(j)] + pair_buf[j // 2, rows(r), :]

    base = wide // 2

    def to_plane(step):
        to = (chip + step) % chips
        return to, remote(
            send_buf.at[to], piece_buf.at[chip],
            dec_send.at[base + step], dec_recv.at[base + step], view, 2 * to + core,
        )

    def plane_out(step, carry):
        to, sending = to_plane(step)
        send_buf[to] = chip_sum(to).astype(jnp.bfloat16)
        sending.start()
        return carry

    lax.fori_loop(1, chips, plane_out, 0)
    piece_buf[chip] = chip_sum(chip).astype(jnp.bfloat16)

    middle = owners // 2
    lax.fori_loop(lead, middle, give, 0)

    def plane_in(step, carry):
        to_plane(step)[1].wait()
        return carry

    lax.fori_loop(1, chips, plane_in, 0)
    total = piece_buf[0].astype(jnp.float32)
    for i in range(1, chips):
        total = total + piece_buf[i].astype(jnp.float32)
    mine_buf[...] = total
    view_buf[view] = total

    def to_view(step):
        return remote(
            mine_buf, view_buf.at[view],
            dec_send.at[base + chips + step], dec_recv.at[base + chips + step],
            (view + step) % n_view, tile,
        )

    for step in range(1, n_view):
        to_view(step).start()
    second = owners
    lax.fori_loop(middle, second, give, 0)
    for step in range(1, n_view):
        to_view(step).wait()
    whole = view_buf[0]
    for i in range(1, n_view):
        whole = whole + view_buf[i]
    p_rows, p_cols = rows(tile // wide), cols(tile % wide)
    dec_ref[p_rows, p_cols] = (whole * scale).astype(dec_ref.dtype)

    after = base + chips + n_view

    def spread_out(step):
        to = (chip + step) % chips
        return remote(
            dec_ref.at[p_rows, p_cols], dec_ref.at[p_rows, p_cols],
            dec_send.at[after + step], dec_recv.at[after + step], view, 2 * to + core,
        )

    def spread_start(step, carry):
        spread_out(step).start()
        return carry

    lax.fori_loop(1, chips, spread_start, 0)
    lax.fori_loop(second, turns, give, 0)
    for r in range(2):
        out_buf[me, r] = block_for(me, r)
    own_copy = pltpu.make_async_copy(out_buf.at[me], recv_ref.at[me], own_sem)
    own_copy.start()

    def spread_wait(step, carry):
        spread_out(step).wait()
        return carry

    lax.fori_loop(1, chips, spread_wait, 0)

    def to_pair_end(i):
        part = dec_ref.at[:, cols(2 * i + core)]
        k = after + chips + i
        return remote(part, part, dec_send.at[k], dec_recv.at[k], view, 2 * chip + 1 - core)

    for i in range(wide // 2):
        to_pair_end(i).start()

    def finish(step, carry):
        copy(step)[2].wait()
        return carry

    lax.fori_loop(0, turns, finish, 0)
    own_copy.wait()
    for i in range(wide // 2):
        to_pair_end(i).wait()


def train(slot, listed, tile_w, arrived, decoder, target, scale):
    n_view, n_tile = lax.axis_size("view"), lax.axis_size("tile")
    owners = n_view * n_tile
    pixels = tile_w.shape[0]
    chans = arrived.shape[2]
    deep, outs = decoder.shape
    wide = outs // chans
    high = deep * wide // n_tile
    copies = wide // 2 + n_tile // 2 + n_view + n_tile // 2 + wide // 2
    vmem = pl.BlockSpec(memory_space=pltpu.VMEM)
    smem = pl.BlockSpec(memory_space=pltpu.SMEM)
    hbm = pl.BlockSpec(memory_space=pl.ANY)
    groups = tile_w.shape[1] // (GROUP * chans)
    return pl.pallas_call(
        functools.partial(train_kernel, scale),
        in_specs=[smem, smem, hbm, hbm, hbm, hbm],
        out_specs=[hbm, vmem],
        out_shape=[
            jax.ShapeDtypeStruct((owners, 2, chans, chans), jnp.bfloat16),
            jax.ShapeDtypeStruct((deep, outs), jnp.bfloat16),
        ],
        scratch_shapes=[
            pltpu.VMEM(tile_w.shape, tile_w.dtype),
            pltpu.VMEM(arrived.shape, arrived.dtype),
            pltpu.VMEM(decoder.shape, decoder.dtype),
            pltpu.VMEM((pixels, chans), jnp.float32),
            pltpu.VMEM((pixels + 4 * chans, chans), jnp.bfloat16),
            pltpu.VMEM((pixels + 2 * chans, outs), jnp.bfloat16),
            pltpu.VMEM((deep, outs), jnp.float32),
            pltpu.VMEM((owners, 2, chans, chans), jnp.bfloat16),
            pltpu.VMEM((wide // 2, deep, chans), jnp.float32),
            pltpu.VMEM((high, chans), jnp.float32),
            pltpu.VMEM((n_tile // 2, high, chans), jnp.bfloat16),
            pltpu.VMEM((n_tile // 2, high, chans), jnp.bfloat16),
            pltpu.VMEM((n_view, high, chans), jnp.float32),
            pltpu.SemaphoreType.DMA((2 * owners,)),
            pltpu.SemaphoreType.DMA((2 * owners,)),
            pltpu.SemaphoreType.DMA((copies,)),
            pltpu.SemaphoreType.DMA((copies,)),
            pltpu.SemaphoreType.DMA((4,)),
            pltpu.SemaphoreType.DMA((4,)),
            pltpu.SemaphoreType.DMA,
            pltpu.SemaphoreType.DMA((8,)),
            pltpu.SemaphoreType.DMA((groups,)),
            pltpu.SemaphoreType.DMA((2,)),
        ],
        compiler_params=pltpu.CompilerParams(
            collective_id=0, has_side_effects=True, vmem_limit_bytes=58 << 20
        ),
    )(slot, listed, tile_w, arrived, decoder, target)


def add_kernel(idx_ref, in_ref, dec_in_ref, out_ref, dec_out_ref, buf, acc, dec_buf, in_sem, out_sem, dec_sem):
    count = in_ref.shape[0]
    owned = out_ref.shape[0]
    loads, stores = in_sem.shape[0], out_sem.shape[0]
    per, back = count // loads, owned // stores

    def load(i):
        return pltpu.make_async_copy(
            in_ref.at[pl.ds(i * per, per)], buf.at[pl.ds(i * per, per)], in_sem.at[i]
        )

    def store(i):
        return pltpu.make_async_copy(
            acc.at[pl.ds(i * back, back)], out_ref.at[pl.ds(i * back, back)], out_sem.at[i]
        )

    for i in range(loads):
        load(i).start()
    dec_in = pltpu.make_async_copy(dec_in_ref, dec_buf, dec_sem.at[0])
    dec_in.start()
    acc[...] = jnp.zeros_like(acc)

    for i in range(loads):
        load(i).wait()

        def one(j, carry):
            where = idx_ref[j]

            @pl.when(where >= 0)
            def _():
                acc[where] += buf[j].astype(jnp.float32)

            return carry

        lax.fori_loop(i * per, (i + 1) * per, one, 0, unroll=8)

    for i in range(stores):
        store(i).start()
    dec_in.wait()
    dec_out = pltpu.make_async_copy(dec_buf, dec_out_ref, dec_sem.at[1])
    dec_out.start()
    for i in range(stores):
        store(i).wait()
    dec_out.wait()


def add_up(index, received, decoder_grad, owned):
    count, block, chans = received.shape
    loads, stores = 16, 8
    hbm = pl.BlockSpec(memory_space=pl.ANY)
    return pl.pallas_call(
        add_kernel,
        in_specs=[pl.BlockSpec(memory_space=pltpu.SMEM), hbm, hbm],
        out_specs=[hbm, hbm],
        scratch_shapes=[
            pltpu.VMEM((count, block, chans), received.dtype),
            pltpu.VMEM((owned, block, chans), jnp.float32),
            pltpu.VMEM(decoder_grad.shape, decoder_grad.dtype),
            pltpu.SemaphoreType.DMA((loads,)),
            pltpu.SemaphoreType.DMA((stores,)),
            pltpu.SemaphoreType.DMA((2,)),
        ],
        out_shape=[
            jax.ShapeDtypeStruct((owned, block, chans), jnp.float32),
            jax.ShapeDtypeStruct(decoder_grad.shape, decoder_grad.dtype),
        ],
        compiler_params=pltpu.CompilerParams(vmem_limit_bytes=56 << 20),
    )(index, received, decoder_grad)


def body(features, block_ids, weights, decoder, target):
    n_view = lax.axis_size("view")
    n_tile = lax.axis_size("tile")
    owners = n_view * n_tile
    g_dev, block, chans = features.shape
    rows, width, listed = (weights.shape[1], weights.shape[2], weights.shape[3])
    k_len = block_ids.shape[2]
    cap = 2 * k_len // owners
    pixels = rows * width
    ids = block_ids[0, 0]
    owner = ids // g_dev
    local = ids - owner * g_dev
    positions = jnp.arange(k_len)
    before = positions[None, :] < positions[:, None]
    rank = jnp.sum(((owner[:, None] == owner[None, :]) & before).astype(jnp.int32), axis=1)
    slot = owner * cap + rank
    place = slot[None, :] == jnp.arange(owners * cap)[:, None]
    request = jnp.sum(jnp.where(place, local[None, :] + 1, 0), axis=1).reshape(owners, cap) - 1
    incoming = lax.all_to_all(request, ("view", "tile"), split_axis=0, concat_axis=0, tiled=True)
    incoming = incoming.reshape(-1)
    outgoing = pick(jnp.maximum(incoming, 0), features).reshape(owners, cap, block, chans)
    arrived = lax.all_to_all(outgoing, ("view", "tile"), split_axis=0, concat_axis=0, tiled=True)
    arrived = arrived.reshape(owners * cap, block, chans)
    tile_w = weights.reshape(pixels, listed)
    scale = 1.0 / math.sqrt(n_view * n_tile * pixels)
    in_slot = jnp.sum(jnp.where(place, positions[None, :], 0), axis=1)
    received, decoder_grad = train(
        slot, in_slot, tile_w, arrived, decoder, target.reshape(pixels, -1), scale
    )
    received = received.reshape(owners * cap, block, chans)
    return tuple(add_up(incoming, received, decoder_grad, g_dev))


def solution(mesh):
    placed = (
        P(("view", "tile"), None, None),
        P("view", "tile", None),
        P("view", "tile", None, None),
        P(),
        P("view", "tile", None, None),
    )
    return jax.shard_map(
        body,
        mesh=mesh,
        in_specs=placed,
        out_specs=(P(("view", "tile"), None, None), P()),
        check_vma=False,
    )
```

```python
import functools
import math

import jax
import jax.numpy as jnp
from jax import lax
from jax.experimental import pallas as pl
from jax.experimental.pallas import tpu as pltpu
from jax.sharding import PartitionSpec as P

GROUP = 8


def pick_kernel(idx_ref, feat_ref, out_ref):
    step = pl.program_id(0)
    count = out_ref.shape[0]
    for j in range(count):
        out_ref[j] = feat_ref[idx_ref[step * count + j]]


def pick(index, features):
    count = index.shape[0]
    per = 16
    tail = features.shape[1:]
    return pl.pallas_call(
        pick_kernel,
        grid_spec=pltpu.PrefetchScalarGridSpec(
            num_scalar_prefetch=1,
            grid=(count // per,),
            in_specs=[pl.BlockSpec(memory_space=pltpu.VMEM)],
            out_specs=pl.BlockSpec((per, *tail), lambda i, idx: (i, 0, 0)),
        ),
        out_shape=jax.ShapeDtypeStruct((count, *tail), features.dtype),
        compiler_params=pltpu.CompilerParams(vmem_limit_bytes=16 << 20),
    )(index, features)


def at_offset(step, n_view, n_tile):
    view, tile = lax.axis_index("view"), lax.axis_index("tile")
    side = n_view
    rem, div = lax.rem, lax.div
    half = n_view * n_tile // 2
    rest = rem(step, half)
    first, second, third = rem(rest, side), rem(div(rest, side), side), div(rest, side * side)
    core = rem(div(step, half) + step, 2)
    y, x, c = div(tile, 2 * side), rem(div(tile, 2), side), rem(tile, 2)
    to_y = rem(y + first + second, side)
    to_x = rem(x + first + third + 2 * second, side)
    return rem(view + first, side), (to_y * side + to_x) * 2 + rem(c + core, 2)


def train_kernel(
    scale, slot_ref, listed_ref, w_hbm, arrived_hbm, dec_w_hbm, target_hbm, recv_ref, dec_ref,
    w_ref, arrived_ref, dec_w_ref, acc, rows_buf, target_buf, part_ref,
    out_buf, pair_buf, mine_buf, piece_buf, send_buf, view_buf,
    send_sem, recv_sem, dec_send, dec_recv, halo_send, halo_recv, own_sem,
    block_sem, weight_sem, other_sem,
):
    n_view, n_tile = lax.axis_size("view"), lax.axis_size("tile")
    owners = n_view * n_tile
    chips = n_tile // 2
    view, tile = lax.axis_index("view"), lax.axis_index("tile")
    me = view * n_tile + tile
    chip, core = tile // 2, tile % 2
    block = recv_ref.shape[3]
    high = piece_buf.shape[1]
    wide = part_ref.shape[1] // block
    pixels = w_ref.shape[0]
    width = block

    def remote(src, dst, send, recv, v, t):
        return pltpu.make_async_remote_copy(
            src_ref=src, dst_ref=dst, send_sem=send, recv_sem=recv,
            device_id=(v, t), device_id_type=pl.DeviceIdType.MESH,
        )

    def cols(j):
        return pl.ds(pl.multiple_of(j * block, block), block)

    def rows(j):
        return pl.ds(pl.multiple_of(j * high, 16), high)

    group = GROUP * block
    groups = w_ref.shape[1] // group
    few = arrived_ref.shape[0] // block_sem.shape[0]

    def block_load(i):
        part = pl.ds(i * few, few)
        return pltpu.make_async_copy(arrived_hbm.at[part], arrived_ref.at[part], block_sem.at[i])

    def weight_load(i):
        part = pl.ds(pl.multiple_of(i * group, group), group)
        return pltpu.make_async_copy(w_hbm.at[:, part], w_ref.at[:, part], weight_sem.at[i])

    others = [
        pltpu.make_async_copy(dec_w_hbm, dec_w_ref, other_sem.at[0]),
        pltpu.make_async_copy(target_hbm, target_buf.at[pl.ds(width, pixels)], other_sem.at[1]),
    ]
    for i in range(block_sem.shape[0]):
        block_load(i).start()
    for i in range(groups):
        weight_load(i).start()
    for one in others:
        one.start()

    barrier = pltpu.get_barrier_semaphore()

    def greet(step, carry):
        v = lax.rem(view + lax.div(step, n_tile), n_view)
        t = lax.rem(tile + lax.rem(step, n_tile), n_tile)
        pl.semaphore_signal(
            barrier, inc=1, device_id=(v, t), device_id_type=pl.DeviceIdType.MESH
        )
        return carry

    lax.fori_loop(1, owners, greet, 0)

    right, left = (tile + 1) % n_tile, (tile + n_tile - 1) % n_tile
    two = 2 * width

    def halo(buf, i, src, size, dst, to):
        return remote(
            buf.at[pl.ds(src, size)], buf.at[pl.ds(dst, size)],
            halo_send.at[i], halo_recv.at[i], view, to,
        )

    target_halos = [
        halo(target_buf, 0, pixels, width, 0, right),
        halo(target_buf, 1, width, width, width + pixels, left),
    ]
    acc[...] = jnp.zeros_like(acc)
    for i in range(block_sem.shape[0]):
        block_load(i).wait()

    def add_group(i, carry):
        weight_load(i).wait()
        stacked = jnp.concatenate(
            [arrived_ref[slot_ref[i * GROUP + j]] for j in range(GROUP)], axis=0
        )
        columns = pl.ds(pl.multiple_of(i * group, group), group)
        acc[...] += jnp.dot(w_ref[:, columns], stacked, preferred_element_type=jnp.float32)
        return carry

    lax.fori_loop(0, groups, add_group, 0)
    for one in others:
        one.wait()
    rows_buf[two : two + pixels, :] = acc[...].astype(jnp.bfloat16)
    image_halos = [
        halo(rows_buf, 2, pixels, two, 0, right),
        halo(rows_buf, 3, two, two, two + pixels, left),
    ]
    pl.semaphore_wait(barrier, owners - 1)
    for one in image_halos + target_halos:
        one.start()
    for one in image_halos + target_halos:
        one.wait()

    padded = pixels + 4 * width
    first, last = tile == 0, tile == n_tile - 1
    place = lax.broadcasted_iota(jnp.int32, (padded, block), 0)
    outside = (first & (place < two)) | (last & (place >= two + pixels))
    image = jnp.where(outside, 0.0, rows_buf[...].astype(jnp.float32))
    column = place % width
    before = jnp.where(column == 0, 0.0, pltpu.roll(image, 1, 0))
    after_px = jnp.where(column == width - 1, 0.0, pltpu.roll(image, padded - 1, 0))
    shifted = jnp.concatenate(
        [a.astype(jnp.bfloat16) for a in (before, image, after_px)], axis=1
    )
    trans = jnp.concatenate(
        [a.T.astype(jnp.bfloat16) for a in (before, image, after_px)], axis=0
    )
    outs = dec_w_ref.shape[1]
    deep = 3 * block
    inner = pixels + two
    decoded = -target_buf[...].astype(jnp.float32)
    for dy in range(3):
        decoded = decoded + jnp.dot(
            shifted[dy * width : dy * width + inner], dec_w_ref[dy * deep : (dy + 1) * deep, :],
            preferred_element_type=jnp.float32,
        )
    place = lax.broadcasted_iota(jnp.int32, (inner, outs), 0)
    outside = (first & (place < width)) | (last & (place >= width + pixels))
    dout = jnp.where(outside, 0.0, decoded).astype(jnp.bfloat16)
    own = dout[width : width + pixels]
    for dy in range(3):
        low = (1 + dy) * width
        part_ref[dy * deep : (dy + 1) * deep, :] = jnp.dot(
            trans[:, low : low + pixels], own, preferred_element_type=jnp.float32
        )

    def to_pair(i):
        return remote(
            part_ref.at[:, cols(2 * i + 1 - core)], pair_buf.at[i],
            dec_send.at[i], dec_recv.at[i], view, 2 * chip + 1 - core,
        )

    for i in range(wide // 2):
        to_pair(i).start()

    spread = jnp.zeros((pixels, deep), jnp.float32)
    for dy in range(3):
        low = (2 - dy) * width
        spread = spread + lax.dot_general(
            dout[low : low + pixels], dec_w_ref[dy * deep : (dy + 1) * deep, :],
            (((1,), (1,)), ((), ())), preferred_element_type=jnp.float32,
        )
    column = lax.broadcasted_iota(jnp.int32, (pixels, block), 0) % width
    later = jnp.where(column == width - 1, 0.0, pltpu.roll(spread[:, :block], pixels - 1, 0))
    earlier = jnp.where(column == 0, 0.0, pltpu.roll(spread[:, 2 * block :], 1, 0))
    image_grad = (later + spread[:, block : 2 * block] + earlier).astype(jnp.bfloat16)
    flipped = image_grad.astype(jnp.float32).T.astype(jnp.bfloat16)

    def block_for(lin, r):
        some = w_ref[:, pl.ds(listed_ref[2 * lin + r] * block, block)]
        return jnp.dot(flipped, some, preferred_element_type=jnp.float32).T.astype(jnp.bfloat16)

    def copy(turn):
        step = lax.rem(turn, owners - 1) + 1
        r = lax.div(turn, owners - 1)
        v, t = at_offset(step, n_view, n_tile)
        lin = v * n_tile + t
        return lin, r, remote(
            out_buf.at[lin, r], recv_ref.at[me, r], send_sem.at[turn], recv_sem.at[turn], v, t
        )

    def give(turn, carry):
        lin, r, sending = copy(turn)
        out_buf[lin, r] = block_for(lin, r)
        sending.start()
        return carry

    turns = 2 * (owners - 1)

    lead = 16
    lax.fori_loop(0, lead, give, 0)
    for i in range(wide // 2):
        to_pair(i).wait()

    def chip_sum(p_chip):
        p = 2 * p_chip + core
        r, j = p // wide, p % wide
        return part_ref[rows(r), cols(j)] + pair_buf[j // 2, rows(r), :]

    base = wide // 2

    def to_plane(step):
        to = (chip + step) % chips
        return to, remote(
            send_buf.at[to], piece_buf.at[chip],
            dec_send.at[base + step], dec_recv.at[base + step], view, 2 * to + core,
        )

    def plane_out(step, carry):
        to, sending = to_plane(step)
        send_buf[to] = chip_sum(to).astype(jnp.bfloat16)
        sending.start()
        return carry

    lax.fori_loop(1, chips, plane_out, 0)
    piece_buf[chip] = chip_sum(chip).astype(jnp.bfloat16)

    middle = owners // 2
    lax.fori_loop(lead, middle, give, 0)

    def plane_in(step, carry):
        to_plane(step)[1].wait()
        return carry

    lax.fori_loop(1, chips, plane_in, 0)
    total = piece_buf[0].astype(jnp.float32)
    for i in range(1, chips):
        total = total + piece_buf[i].astype(jnp.float32)
    mine_buf[...] = total
    view_buf[view] = total

    def to_view(step):
        return remote(
            mine_buf, view_buf.at[view],
            dec_send.at[base + chips + step], dec_recv.at[base + chips + step],
            (view + step) % n_view, tile,
        )

    for step in range(1, n_view):
        to_view(step).start()
    second = owners
    lax.fori_loop(middle, second, give, 0)
    for step in range(1, n_view):
        to_view(step).wait()
    whole = view_buf[0]
    for i in range(1, n_view):
        whole = whole + view_buf[i]
    p_rows, p_cols = rows(tile // wide), cols(tile % wide)
    dec_ref[p_rows, p_cols] = (whole * scale).astype(dec_ref.dtype)

    after = base + chips + n_view

    def spread_out(step):
        to = (chip + step) % chips
        return remote(
            dec_ref.at[p_rows, p_cols], dec_ref.at[p_rows, p_cols],
            dec_send.at[after + step], dec_recv.at[after + step], view, 2 * to + core,
        )

    def spread_start(step, carry):
        spread_out(step).start()
        return carry

    lax.fori_loop(1, chips, spread_start, 0)
    lax.fori_loop(second, turns, give, 0)
    for r in range(2):
        out_buf[me, r] = block_for(me, r)
    own_copy = pltpu.make_async_copy(out_buf.at[me], recv_ref.at[me], own_sem)
    own_copy.start()

    def spread_wait(step, carry):
        spread_out(step).wait()
        return carry

    lax.fori_loop(1, chips, spread_wait, 0)

    def to_pair_end(i):
        part = dec_ref.at[:, cols(2 * i + core)]
        k = after + chips + i
        return remote(part, part, dec_send.at[k], dec_recv.at[k], view, 2 * chip + 1 - core)

    for i in range(wide // 2):
        to_pair_end(i).start()

    def finish(step, carry):
        copy(step)[2].wait()
        return carry

    lax.fori_loop(0, turns, finish, 0)
    own_copy.wait()
    for i in range(wide // 2):
        to_pair_end(i).wait()


def train(slot, listed, tile_w, arrived, decoder, target, scale):
    n_view, n_tile = lax.axis_size("view"), lax.axis_size("tile")
    owners = n_view * n_tile
    pixels = tile_w.shape[0]
    chans = arrived.shape[2]
    deep, outs = decoder.shape
    wide = outs // chans
    high = deep * wide // n_tile
    copies = wide // 2 + n_tile // 2 + n_view + n_tile // 2 + wide // 2
    vmem = pl.BlockSpec(memory_space=pltpu.VMEM)
    smem = pl.BlockSpec(memory_space=pltpu.SMEM)
    hbm = pl.BlockSpec(memory_space=pl.ANY)
    groups = tile_w.shape[1] // (GROUP * chans)
    return pl.pallas_call(
        functools.partial(train_kernel, scale),
        in_specs=[smem, smem, hbm, hbm, hbm, hbm],
        out_specs=[hbm, vmem],
        out_shape=[
            jax.ShapeDtypeStruct((owners, 2, chans, chans), jnp.bfloat16),
            jax.ShapeDtypeStruct((deep, outs), jnp.bfloat16),
        ],
        scratch_shapes=[
            pltpu.VMEM(tile_w.shape, tile_w.dtype),
            pltpu.VMEM(arrived.shape, arrived.dtype),
            pltpu.VMEM(decoder.shape, decoder.dtype),
            pltpu.VMEM((pixels, chans), jnp.float32),
            pltpu.VMEM((pixels + 4 * chans, chans), jnp.bfloat16),
            pltpu.VMEM((pixels + 2 * chans, outs), jnp.bfloat16),
            pltpu.VMEM((deep, outs), jnp.float32),
            pltpu.VMEM((owners, 2, chans, chans), jnp.bfloat16),
            pltpu.VMEM((wide // 2, deep, chans), jnp.float32),
            pltpu.VMEM((high, chans), jnp.float32),
            pltpu.VMEM((n_tile // 2, high, chans), jnp.bfloat16),
            pltpu.VMEM((n_tile // 2, high, chans), jnp.bfloat16),
            pltpu.VMEM((n_view, high, chans), jnp.float32),
            pltpu.SemaphoreType.DMA((2 * owners,)),
            pltpu.SemaphoreType.DMA((2 * owners,)),
            pltpu.SemaphoreType.DMA((copies,)),
            pltpu.SemaphoreType.DMA((copies,)),
            pltpu.SemaphoreType.DMA((4,)),
            pltpu.SemaphoreType.DMA((4,)),
            pltpu.SemaphoreType.DMA,
            pltpu.SemaphoreType.DMA((8,)),
            pltpu.SemaphoreType.DMA((groups,)),
            pltpu.SemaphoreType.DMA((2,)),
        ],
        compiler_params=pltpu.CompilerParams(
            collective_id=0, has_side_effects=True, vmem_limit_bytes=58 << 20
        ),
    )(slot, listed, tile_w, arrived, decoder, target)


def add_kernel(idx_ref, in_ref, dec_in_ref, out_ref, dec_out_ref, buf, acc, dec_buf, in_sem, out_sem, dec_sem):
    count = in_ref.shape[0]
    owned = out_ref.shape[0]
    loads, stores = in_sem.shape[0], out_sem.shape[0]
    per, back = count // loads, owned // stores

    def load(i):
        return pltpu.make_async_copy(
            in_ref.at[pl.ds(i * per, per)], buf.at[pl.ds(i * per, per)], in_sem.at[i]
        )

    def store(i):
        return pltpu.make_async_copy(
            acc.at[pl.ds(i * back, back)], out_ref.at[pl.ds(i * back, back)], out_sem.at[i]
        )

    for i in range(loads):
        load(i).start()
    dec_in = pltpu.make_async_copy(dec_in_ref, dec_buf, dec_sem.at[0])
    dec_in.start()
    acc[...] = jnp.zeros_like(acc)

    for i in range(loads):
        load(i).wait()

        def one(j, carry):
            where = idx_ref[j]

            @pl.when(where >= 0)
            def _():
                acc[where] += buf[j].astype(jnp.float32)

            return carry

        lax.fori_loop(i * per, (i + 1) * per, one, 0, unroll=8)

    for i in range(stores):
        store(i).start()
    dec_in.wait()
    dec_out = pltpu.make_async_copy(dec_buf, dec_out_ref, dec_sem.at[1])
    dec_out.start()
    for i in range(stores):
        store(i).wait()
    dec_out.wait()


def add_up(index, received, decoder_grad, owned):
    count, block, chans = received.shape
    loads, stores = 16, 8
    hbm = pl.BlockSpec(memory_space=pl.ANY)
    return pl.pallas_call(
        add_kernel,
        in_specs=[pl.BlockSpec(memory_space=pltpu.SMEM), hbm, hbm],
        out_specs=[hbm, hbm],
        scratch_shapes=[
            pltpu.VMEM((count, block, chans), received.dtype),
            pltpu.VMEM((owned, block, chans), jnp.float32),
            pltpu.VMEM(decoder_grad.shape, decoder_grad.dtype),
            pltpu.SemaphoreType.DMA((loads,)),
            pltpu.SemaphoreType.DMA((stores,)),
            pltpu.SemaphoreType.DMA((2,)),
        ],
        out_shape=[
            jax.ShapeDtypeStruct((owned, block, chans), jnp.float32),
            jax.ShapeDtypeStruct(decoder_grad.shape, decoder_grad.dtype),
        ],
        compiler_params=pltpu.CompilerParams(vmem_limit_bytes=56 << 20),
    )(index, received, decoder_grad)


def body(features, block_ids, weights, decoder, target):
    n_view = lax.axis_size("view")
    n_tile = lax.axis_size("tile")
    owners = n_view * n_tile
    g_dev, block, chans = features.shape
    rows, width, listed = (weights.shape[1], weights.shape[2], weights.shape[3])
    k_len = block_ids.shape[2]
    cap = 2 * k_len // owners
    pixels = rows * width
    ids = block_ids[0, 0]
    owner = ids // g_dev
    local = ids - owner * g_dev
    positions = jnp.arange(k_len)
    before = positions[None, :] < positions[:, None]
    rank = jnp.sum(((owner[:, None] == owner[None, :]) & before).astype(jnp.int32), axis=1)
    slot = owner * cap + rank
    place = slot[None, :] == jnp.arange(owners * cap)[:, None]
    request = jnp.sum(jnp.where(place, local[None, :] + 1, 0), axis=1).reshape(owners, cap) - 1
    incoming = lax.all_to_all(request, ("view", "tile"), split_axis=0, concat_axis=0, tiled=True)
    incoming = incoming.reshape(-1)
    outgoing = pick(jnp.maximum(incoming, 0), features).reshape(owners, cap, block, chans)
    arrived = lax.all_to_all(outgoing, ("view", "tile"), split_axis=0, concat_axis=0, tiled=True)
    arrived = arrived.reshape(owners * cap, block, chans)
    tile_w = weights.reshape(pixels, listed)
    scale = 1.0 / math.sqrt(n_view * n_tile * pixels)
    in_slot = jnp.sum(jnp.where(place, positions[None, :], 0), axis=1)
    received, decoder_grad = train(
        slot, in_slot, tile_w, arrived, decoder, target.reshape(pixels, -1), scale
    )
    received = received.reshape(owners * cap, block, chans)
    return tuple(add_up(incoming, received, decoder_grad, g_dev))


def solution(mesh):
    placed = (
        P(("view", "tile"), None, None),
        P("view", "tile", None),
        P("view", "tile", None, None),
        P(),
        P("view", "tile", None, None),
    )
    return jax.shard_map(
        body,
        mesh=mesh,
        in_specs=placed,
        out_specs=(P(("view", "tile"), None, None), P()),
        check_vma=False,
    )
```
